256 devices in a mesh: wide: 64 (over x, y_hi, z), narrow: 4 (over y_lo, core).
Axes of the slice: x: 4, y: 4 (y_hi: 2, y_lo: 2; y = y_hi * 2 + y_lo), z: 8, core: 2. Of those that a mesh axis runs over, the one named last changes fastest.
Arguments:
- image_features: bfloat16 [49152, 1152], P(('wide', 'narrow')), may hold values from -6 to 6
- text_features: bfloat16 [49152, 1152], P(('wide', 'narrow')), may hold values from -6 to 6
- image_weight: bfloat16 [1152, 1152], replicated, may hold values from -0.1875 to 0.1875
- text_weight: bfloat16 [1152, 1152], replicated, may hold values from -0.1875 to 0.1875
- partner: int32 [64, 768], P('wide', 'narrow'), may hold values from 0 to 767, each once within a row
Outputs:
- image_feature_grad: bfloat16 [49152, 1152], P(('wide', 'narrow'))
- text_feature_grad: bfloat16 [49152, 1152], P(('wide', 'narrow'))
- image_weight_grad: float32 [1152, 1152], P('wide', 'narrow')
- text_weight_grad: float32 [1152, 1152], P('wide', 'narrow')
The draws below stay inside these ranges and needn't reach their ends.
Inputs may be any that keep to these rules, and one draw needn't show every extreme that they name: `partner`: each row is a permutation: every caption of a group belongs to exactly one image of that group.
All inputs are finite; a program needn't handle non-finite values.
Results may differ from the reference program's by a relative error of at most 0.007.
Values may be sent and summed in bfloat16 or wider, within the bound.
A program may use at most 128 MiB of HBM per device.

```python
import jax
import jax.numpy as jnp
from jax import lax

D = 1152
E = 1152
GROUP = 768
TOKENS = 49152
N_WIDE = 64


def strengthened(entries, rng, source, target, parts, factor):
    def block_of(dim):
        return (jnp.arange(entries.shape[dim]) // (entries.shape[dim] // parts)).reshape((-1,) + (1,) * (entries.ndim - 1 - dim))

    near = jax.random.permutation(rng, parts)[block_of(target)]
    other_side = (block_of(target) + parts // 2) % parts
    return jnp.where((block_of(source) == near) | (block_of(source) == other_side), factor * entries, entries)


def steps_of(stream_key, extent, split, low, top_value):
    def one(position, parts):
        heights = jax.random.uniform(jax.random.fold_in(jax.random.fold_in(stream_key, 6), position), (parts,), jnp.float32, low / len(split), top_value / len(split))
        return jnp.repeat(jnp.exp(heights), extent[position] // parts).reshape((-1,) + (1,) * (len(extent) - position - 1))

    gain = one(*split[0])
    for cut in split[1:]:
        gain = gain * one(*cut)
    return gain


def gaussian(key, shape, spread, most, split=(), kind=jnp.bfloat16):
    gain = steps_of(key, shape, split, -0.22, 0.18) if split else 1.0
    array = jax.random.normal(key, shape, jnp.float32) * spread * gain
    return jnp.minimum(jnp.maximum(array, -most), most).astype(kind)


def noise_with(own_key, shape, spread, reach, cuts, heavy, kind=jnp.bfloat16):
    drawn = spread * jax.random.normal(own_key, shape, jnp.float32)
    if cuts:
        drawn = drawn * steps_of(own_key, shape, cuts, -0.22, 0.18)
    return jnp.clip(strengthened(drawn, jax.random.fold_in(own_key, 3), *heavy), -reach, reach).astype(kind)


def setup_inputs(seed: int = 0) -> dict:
    splits = jax.random.split(jax.random.key(seed), 6)
    image_features = noise_with(splits[0], (TOKENS, D), 0.25, 6.0, ((0, 256),), (0, 1, 128, 5.5))
    text_features = noise_with(splits[1], (TOKENS, D), 0.25, 6.0, ((0, 256),), (0, 1, 128, 5.5))
    image_weight = gaussian(splits[2], (D, E), D ** -0.5, 0.1875)
    text_weight = gaussian(splits[3], (D, E), D ** -0.5, 0.1875)
    partner = jax.vmap(lambda own: jax.random.permutation(own, GROUP))(jax.random.split(splits[4], N_WIDE)).reshape((N_WIDE, GROUP)).astype(jnp.int32)
    return dict(image_features=image_features, text_features=text_features, image_weight=image_weight, text_weight=text_weight, partner=partner)


logit_scale = 10.0
logit_bias = -2.0
norm_eps = 1e-06

def embed(features, weight):
    proj = jnp.dot(features, weight, preferred_element_type=jnp.float32)
    inverse = lax.rsqrt(lax.optimization_barrier(jnp.sum(proj * proj, axis=1, keepdims=True)) + norm_eps)
    return (proj, inverse, (proj * inverse).astype(jnp.bfloat16))

def pair_terms(left, right, match):
    logits = logit_scale * lax.dot_general(left, right, (((1,), (1,)), ((), ())), preferred_element_type=jnp.float32) + logit_bias
    signs = jnp.where(match, 1.0, -1.0).astype(jnp.float32)
    return (-logit_scale * signs * jax.nn.sigmoid(-signs * logits)).astype(jnp.bfloat16)

def proj_backward(proj, inverse, grad):
    along = lax.optimization_barrier(jnp.sum(proj * grad, axis=1, keepdims=True))
    return (inverse * grad - proj * (inverse * inverse * inverse) * along).astype(jnp.bfloat16)

def reference(image_features, text_features, image_weight, text_weight, partner):
    image_proj, image_inv, image_emb = embed(image_features, image_weight)
    text_proj, text_inv, text_emb = embed(text_features, text_weight)
    columns = jnp.arange(GROUP, dtype=jnp.int32)

    def group_grads(items):
        image_rows, text_rows, partner_row = items
        pair_grad = pair_terms(image_rows, text_rows, partner_row[:, None] == columns[None, :])
        image_part = jnp.dot(pair_grad, text_rows, preferred_element_type=jnp.float32)
        text_part = lax.dot_general(pair_grad, image_rows, (((0,), (0,)), ((), ())), preferred_element_type=jnp.float32)
        return (image_part, text_part)
    width = image_emb.shape[1]
    image_grad, text_grad = lax.map(group_grads, (image_emb.reshape(N_WIDE, GROUP, width), text_emb.reshape(N_WIDE, GROUP, width), partner))
    image_grad = image_grad.reshape(TOKENS, width)
    text_grad = text_grad.reshape(TOKENS, width)
    image_pg = proj_backward(image_proj, image_inv, image_grad)
    text_pg = proj_backward(text_proj, text_inv, text_grad)
    image_feature_grad = lax.dot_general(image_pg, image_weight, (((1,), (1,)), ((), ())), preferred_element_type=jnp.float32).astype(jnp.bfloat16)
    text_feature_grad = lax.dot_general(text_pg, text_weight, (((1,), (1,)), ((), ())), preferred_element_type=jnp.float32).astype(jnp.bfloat16)
    image_weight_grad = lax.dot_general(image_features, image_pg, (((0,), (0,)), ((), ())), preferred_element_type=jnp.float32)
    text_weight_grad = lax.dot_general(text_features, text_pg, (((0,), (0,)), ((), ())), preferred_element_type=jnp.float32)
    return (image_feature_grad, text_feature_grad, image_weight_grad, text_weight_grad)
```

```python
import functools

import jax
import jax.numpy as jnp
from jax import lax
from jax.experimental import pallas as pl
from jax.experimental.pallas import tpu as pltpu
from jax.sharding import PartitionSpec as P

logit_scale = 10.0
logit_bias = -2.0
norm_eps = 1e-06

NX, NYH = 4, 2
PIECES = 2
WINDOW = 640
CORE_STEP = 512
PART = 384
PART_STEP = 256
PAD = 32

OWN_CORE, OWN_CHIP, FORWARD = 0, PIECES, 2 * PIECES
CORE_SUM = 3 * PIECES
X_RELAY, X_DIRECT, X_BOTH = CORE_SUM + 4, CORE_SUM + 6, CORE_SUM + 8
Y_SUM = CORE_SUM + 10
Z_SUM = Y_SUM + 3


def kernel(nz, f_i, f_t, w_i_hbm, w_t_hbm, partner, fg_i, fg_t, wg_i, wg_t,
           w, ft, proj, inv, grad, emb, pairs, pg, pgp,
           core_out, core_in, relay_out, relay_in, direct_out, direct_in, both_out, both_in, keep, acc,
           y_out, y_in, z_out, z_in, w_sem, p_send, p_recv, send, recv):
    rows, depth = f_i.shape
    width = w.shape[2]
    chunk = depth // NX
    half = chunk // NYH
    mine = half // nz
    quarter = width // 4
    features = (f_i, f_t)
    wide, narrow = lax.axis_index("wide"), lax.axis_index("narrow")
    z, yh, x = lax.rem(wide, nz), lax.rem(wide // nz, NYH), wide // (nz * NYH)
    yl, c = narrow // 2, lax.rem(narrow, 2)

    def device(x=x, yh=yh, z=z, yl=yl, c=c):
        return ((x * NYH + yh) * nz + z, yl * 2 + c)

    core_peer = device(c=1 - c)
    chip_peer = device(yl=1 - yl)
    far_peer = device(yl=1 - yl, c=1 - c)
    block_core, block_chip, block_far = yl * 2 + 1 - c, (1 - yl) * 2 + c, (1 - yl) * 2 + 1 - c
    x_next, x_prev, x_far = lax.rem(x + 1, NX), lax.rem(x + NX - 1, NX), lax.rem(x + 2, NX)
    next_peer, prev_peer = device(x=x_next), device(x=x_prev)
    y_peers = (
        (yh, 1 - yl, device(yh=yh, yl=1 - yl)),
        (1 - yh, yl, device(yh=1 - yh, yl=yl)),
        (1 - yh, 1 - yl, device(yh=1 - yh, yl=1 - yl)),
    )
    z_peers = [(lax.rem(z + d, nz), device(z=lax.rem(z + d, nz))) for d in range(1, nz)]

    loads = []
    for m, src in ((1, w_t_hbm), (0, w_i_hbm)):
        load = pltpu.make_async_copy(src, w.at[m], w_sem.at[m])
        load.start()
        loads.append(load)

    barrier = pltpu.get_barrier_semaphore()
    peers = [core_peer, chip_peer, far_peer, next_peer, prev_peer, y_peers[1][2], y_peers[2][2]]
    peers += [peer for _, peer in z_peers]
    for peer in peers:
        pl.semaphore_signal(barrier, inc=1, device_id=peer, device_id_type=pl.DeviceIdType.MESH)

    def remote(src, dst, m, s, peer):
        return pltpu.make_async_remote_copy(
            src_ref=src, dst_ref=dst, send_sem=send.at[m, s], recv_sem=recv.at[m, s],
            device_id=peer, device_id_type=pl.DeviceIdType.MESH)

    started = []

    def go(copy):
        copy.start()
        started.append(copy)
        return copy

    piece = rows // PIECES
    own = {}

    def embed(m):
        p = jnp.dot(features[m][...], w[m], preferred_element_type=jnp.float32)
        i = lax.rsqrt(jnp.sum(p * p, axis=1, keepdims=True) + norm_eps)
        proj[m] = p
        inv[m] = i
        emb[m, narrow] = (p * i).astype(jnp.bfloat16)

    def send_own(m):
        for k in range(PIECES):
            ref = emb.at[m, narrow, pl.ds(k * piece, piece)]
            own[m, 0, k] = go(remote(ref, ref, m, OWN_CORE + k, core_peer))
            own[m, 1, k] = go(remote(ref, ref, m, OWN_CHIP + k, chip_peer))

    def forward(m):
        for k in range(PIECES):
            own[m, 1, k].wait_recv()
            ref = emb.at[m, block_chip, pl.ds(k * piece, piece)]
            own[m, 2, k] = go(remote(ref, ref, m, FORWARD + k, core_peer))

    def arrived(m, kind):
        for k in range(PIECES):
            own[m, kind, k].wait_recv()

    loads[0].wait()
    embed(1)
    pl.semaphore_wait(barrier, len(peers))
    send_own(1)
    pairs[narrow] = partner[...]
    pair_copies = []
    for s, peer in enumerate((core_peer, chip_peer, far_peer)):
        copy = pltpu.make_async_remote_copy(
            src_ref=pairs.at[narrow], dst_ref=pairs.at[narrow], send_sem=p_send.at[s], recv_sem=p_recv.at[s],
            device_id=peer, device_id_type=pl.DeviceIdType.MESH)
        pair_copies.append(go(copy))
    loads[1].wait()
    embed(0)
    send_own(0)

    for m in (0, 1):
        ft[m] = features[m][...].T

    down = lax.broadcasted_iota(jnp.int32, (rows, rows), 0)
    along = lax.broadcasted_iota(jnp.int32, (rows, rows), 1)
    partner_down = jnp.sum(
        jnp.where(down == along, partner[...].astype(jnp.float32), 0.0), axis=1, keepdims=True
    ).astype(jnp.int32)

    def add_block(m, block, first):
        other = emb[1 - m, block]
        logits = logit_scale * lax.dot_general(
            emb[m, narrow], other, (((1,), (1,)), ((), ())), preferred_element_type=jnp.float32
        ) + logit_bias
        if m == 0:
            match = partner_down == block * rows + along
        else:
            match = pairs[block] == narrow * rows + down
        pair = jnp.where(match, -logit_scale, logit_scale) * jax.nn.sigmoid(jnp.where(match, -logits, logits))
        part = jnp.dot(pair.astype(jnp.bfloat16), other, preferred_element_type=jnp.float32)
        grad[m] = part if first else grad[m] + part

    def project_back(m):
        p, i, g = proj[m], inv[m], grad[m]
        total = jnp.sum(p * g, axis=1, keepdims=True)
        value = i * g - p * (i * i * i * total)
        pg[m] = value.astype(jnp.bfloat16)
        q = quarter
        moved = jnp.concatenate([value[:, :q], value[:, 2 * q:3 * q], value[:, q:2 * q], value[:, 3 * q:]], axis=1)
        pgp[m] = moved.astype(jnp.bfloat16)

    def feature_grad(m, out):
        out[...] = lax.dot_general(
            pg[m], w[m], (((1,), (1,)), ((), ())), preferred_element_type=jnp.float32
        ).astype(jnp.bfloat16)

    targets = (x_far, x_next, x_prev, x)

    def share(m, xd, core):
        left = ft[m, pl.ds(pl.multiple_of(xd * chunk, 16), chunk), :]
        right = pgp[m, :, pl.ds(pl.multiple_of(core * CORE_STEP, 128), WINDOW)]
        return jnp.dot(left, right, preferred_element_type=jnp.float32)

    core_copies, x_copies, y_copies, z_copies = {}, {}, {}, {}

    def core_start(m):
        for k, xd in enumerate(targets):
            core_out[m, k] = share(m, xd, 1 - c).astype(jnp.bfloat16)
            core_copies[m, k] = go(remote(core_out.at[m, k], core_in.at[m, k], m, CORE_SUM + k, core_peer))

    def chip_share(m, k):
        total = share(m, targets[k], c)
        core_copies[m, k].wait_recv()
        return total + core_in[m, k].astype(jnp.float32)

    def x_send(m, s, out, into, t, peer):
        x_copies[m, s + t] = go(remote(out.at[m, t], into.at[m, t], m, s + t, peer))

    def x_start(m):
        total = chip_share(m, 0)
        for t, peer in enumerate((next_peer, prev_peer)):
            relay_out[m, t] = total[t * half:(t + 1) * half].astype(jnp.bfloat16)
            x_send(m, X_RELAY, relay_out, relay_in, t, peer)
        for t, peer in enumerate((next_peer, prev_peer)):
            total = chip_share(m, 1 + t)
            direct_out[m, t] = total[(1 - t) * half:(2 - t) * half].astype(jnp.bfloat16)
            x_send(m, X_DIRECT, direct_out, direct_in, t, peer)
            keep[m, t] = total[t * half:(t + 1) * half]
        acc[m] = chip_share(m, 3)

    def x_relay(m):
        for t, peer in enumerate((next_peer, prev_peer)):
            x_copies[m, X_RELAY + t].wait_recv()
            both_out[m, t] = (keep[m, t] + relay_in[m, t].astype(jnp.float32)).astype(jnp.bfloat16)
            x_send(m, X_BOTH, both_out, both_in, t, peer)

    def x_finish(m):
        for t in range(2):
            x_copies[m, X_DIRECT + t].wait_recv()
            acc[m, (1 - t) * half:(2 - t) * half] += direct_in[m, t].astype(jnp.float32)
        for t in range(2):
            x_copies[m, X_BOTH + t].wait_recv()
            acc[m, t * half:(t + 1) * half] += both_in[m, t].astype(jnp.float32)

    def y_part(m, h, l):
        return acc[m, pl.ds(pl.multiple_of(h * half, 16), half), pl.ds(pl.multiple_of(l * PART_STEP, 128), PART)]

    def y_start(m):
        for s, (h, l, peer) in enumerate(y_peers):
            y_out[m, s] = y_part(m, h, l).astype(jnp.bfloat16)
            y_copies[m, s] = go(remote(y_out.at[m, s], y_in.at[m, s], m, Y_SUM + s, peer))

    def z_start(m):
        total = y_part(m, yh, yl)
        for s in range(3):
            y_copies[m, s].wait_recv()
            total = total + y_in[m, s].astype(jnp.float32)
        row = lax.broadcasted_iota(jnp.int32, (nz * PAD, half), 0)
        column = lax.broadcasted_iota(jnp.int32, (nz * PAD, half), 1)
        which, within = row // PAD, lax.rem(row, PAD)
        spread = jnp.where((within < mine) & (column == which * mine + within), 1.0, 0.0).astype(jnp.bfloat16)
        padded = jnp.dot(spread, total.astype(jnp.bfloat16), preferred_element_type=jnp.float32).astype(jnp.bfloat16)
        for d in range(nz):
            z_out[m, d] = padded[d * PAD:(d + 1) * PAD]
        for s, (zd, peer) in enumerate(z_peers):
            z_copies[m, s] = go(remote(z_out.at[m, zd], z_in.at[m, s], m, Z_SUM + s, peer))

    def z_finish(m, out):
        total = z_out[m, z].astype(jnp.float32)
        for s in range(nz - 1):
            z_copies[m, s].wait_recv()
            total = total + z_in[m, s].astype(jnp.float32)
        shift = lax.rem(PART - (quarter - PART_STEP) * (yl + 2 * c), PART)
        out[...] = pltpu.roll(total, shift, 1)[:mine, :quarter]

    add = add_block
    add(0, narrow, True)
    pair_copies[0].wait_recv()
    add(1, narrow, True)
    arrived(1, 0)
    add(0, block_core, False)
    arrived(0, 0)
    add(1, block_core, False)

    forward(1)
    add(0, block_chip, False)
    arrived(1, 2)
    add(0, block_far, False)
    project_back(0)
    core_start(0)
    x_start(0)
    feature_grad(0, fg_i)

    forward(0)
    pair_copies[1].wait_recv()
    pair_copies[2].wait_recv()
    add(1, block_chip, False)
    arrived(0, 2)
    add(1, block_far, False)
    project_back(1)
    core_start(1)
    x_relay(0)
    x_start(1)
    x_finish(0)
    y_start(0)
    feature_grad(1, fg_t)
    x_relay(1)
    z_start(0)
    x_finish(1)
    y_start(1)
    z_finish(0, wg_i)
    z_start(1)
    z_finish(1, wg_t)
    for copy in started:
        copy.wait_send()


def local(nz, image_features, text_features, image_weight, text_weight, partner):
    rows, depth = image_features.shape
    width = image_weight.shape[1]
    chunk = depth // NX
    half = chunk // NYH
    mine = half // nz
    b16, f32 = jnp.bfloat16, jnp.float32
    vmem = pl.BlockSpec(memory_space=pltpu.VMEM)
    hbm = pl.BlockSpec(memory_space=pl.ANY)
    copies = Z_SUM + max(nz - 1, 1)
    return pl.pallas_call(
        functools.partial(kernel, nz),
        out_shape=(
            jax.ShapeDtypeStruct((rows, depth), b16),
            jax.ShapeDtypeStruct((rows, depth), b16),
            jax.ShapeDtypeStruct((mine, width // 4), f32),
            jax.ShapeDtypeStruct((mine, width // 4), f32),
        ),
        in_specs=[vmem, vmem, hbm, hbm, vmem],
        out_specs=(vmem,) * 4,
        scratch_shapes=[
            pltpu.VMEM((2, depth, width), b16),
            pltpu.VMEM((2, depth, rows), b16),
            pltpu.VMEM((2, rows, width), f32),
            pltpu.VMEM((2, rows, 1), f32),
            pltpu.VMEM((2, rows, width), f32),
            pltpu.VMEM((2, 4, rows, width), b16),
            pltpu.VMEM((4, 1, rows), jnp.int32),
            pltpu.VMEM((2, rows, width), b16),
            pltpu.VMEM((2, rows, width), b16),
            pltpu.VMEM((2, 4, chunk, WINDOW), b16),
            pltpu.VMEM((2, 4, chunk, WINDOW), b16),
            pltpu.VMEM((2, 2, half, WINDOW), b16),
            pltpu.VMEM((2, 2, half, WINDOW), b16),
            pltpu.VMEM((2, 2, half, WINDOW), b16),
            pltpu.VMEM((2, 2, half, WINDOW), b16),
            pltpu.VMEM((2, 2, half, WINDOW), b16),
            pltpu.VMEM((2, 2, half, WINDOW), b16),
            pltpu.VMEM((2, 2, half, WINDOW), f32),
            pltpu.VMEM((2, chunk, WINDOW), f32),
            pltpu.VMEM((2, 3, half, PART), b16),
            pltpu.VMEM((2, 3, half, PART), b16),
            pltpu.VMEM((2, nz, PAD, PART), b16),
            pltpu.VMEM((2, max(nz - 1, 1), PAD, PART), b16),
            pltpu.SemaphoreType.DMA((2,)),
            pltpu.SemaphoreType.DMA((3,)),
            pltpu.SemaphoreType.DMA((3,)),
            pltpu.SemaphoreType.DMA((2, copies)),
            pltpu.SemaphoreType.DMA((2, copies)),
        ],
        compiler_params=pltpu.CompilerParams(
            collective_id=0, has_side_effects=True, vmem_limit_bytes=56 * 1024 * 1024),
        cost_estimate=pl.CostEstimate(flops=4_500_000_000, bytes_accessed=8_000_000, transcendentals=300_000),
    )(image_features, text_features, image_weight, text_weight, partner)


def solution(mesh):
    in_specs = (
        P(("wide", "narrow"), None),
        P(("wide", "narrow"), None),
        P(),
        P(),
        P("wide", "narrow"),
    )
    out_specs = (
        P(("wide", "narrow"), None),
        P(("wide", "narrow"), None),
        P("wide", "narrow"),
        P("wide", "narrow"),
    )
    nz = mesh.shape["wide"] // (NX * NYH)
    return jax.shard_map(
        functools.partial(local, nz), mesh=mesh, in_specs=in_specs, out_specs=out_specs, check_vma=False)
```

```python
import functools

import jax
import jax.numpy as jnp
from jax import lax
from jax.experimental import pallas as pl
from jax.experimental.pallas import tpu as pltpu
from jax.sharding import PartitionSpec as P

logit_scale = 10.0
logit_bias = -2.0
norm_eps = 1e-06

NX, NYH = 4, 2
PIECES = 2
WINDOW = 640
CORE_STEP = 512
PART = 384
PART_STEP = 256
TILE = 16
Y_FIRST = 64

OWN_CORE, OWN_CHIP, FORWARD = 0, PIECES, 2 * PIECES
CORE_SUM = 3 * PIECES
Z_SUM = CORE_SUM + 4
RINGS = 6


def kernel(nz, f_i, f_t, w_i_hbm, w_t_hbm, partner, fg_i, fg_t, wg_i, wg_t,
           w, ft, proj, inv, grad, emb, pairs, pg, pgp,
           core_out, core_in, acc, sums_i, sums_t, sums_y, last, z_out, z_in, ring_bufs,
           w_sem, p_send, p_recv, send, recv, ring_send, ring_recv):
    rows, depth = f_i.shape
    width = w.shape[2]
    chunk = depth // NX
    half = chunk // NYH
    mine = half // nz
    quarter = width // 4
    features = (f_i, f_t)
    wide, narrow = lax.axis_index("wide"), lax.axis_index("narrow")
    z, yh, x = lax.rem(wide, nz), lax.rem(wide // nz, NYH), wide // (nz * NYH)
    yl, c = narrow // 2, lax.rem(narrow, 2)

    def device(x=x, yh=yh, z=z, yl=yl, c=c):
        return ((x * NYH + yh) * nz + z, yl * 2 + c)

    core_peer = device(c=1 - c)
    chip_peer = device(yl=1 - yl)
    far_peer = device(yl=1 - yl, c=1 - c)
    block_core, block_chip, block_far = yl * 2 + 1 - c, (1 - yl) * 2 + c, (1 - yl) * 2 + 1 - c
    x_next, x_prev, x_far = lax.rem(x + 1, NX), lax.rem(x + NX - 1, NX), lax.rem(x + 2, NX)
    y = yh * 2 + yl
    y_far, y_next, y_prev = lax.rem(y + 2, 4), lax.rem(y + 1, 4), lax.rem(y + 3, 4)
    x_targets = (x_far, x_next, x_prev, x)
    y_targets = (y_far, y_next, y_prev, y)
    x_pair = (device(x=x_next), device(x=x_prev))
    y_pair = tuple(device(yh=t // 2, yl=lax.rem(t, 2)) for t in (y_next, y_prev))
    z_peers = [(lax.rem(z + d, nz), device(z=lax.rem(z + d, nz))) for d in range(1, nz)]

    loads = []
    for m, src in ((1, w_t_hbm), (0, w_i_hbm)):
        load = pltpu.make_async_copy(src, w.at[m], w_sem.at[m])
        load.start()
        loads.append(load)

    barrier = pltpu.get_barrier_semaphore()
    peers = [core_peer, chip_peer, far_peer, *x_pair, device(yh=1 - yh, yl=1 - yl)]
    peers += [peer for _, peer in z_peers]
    for peer in peers:
        pl.semaphore_signal(barrier, inc=1, device_id=peer, device_id_type=pl.DeviceIdType.MESH)

    def remote(src, dst, m, s, peer):
        return pltpu.make_async_remote_copy(
            src_ref=src, dst_ref=dst, send_sem=send.at[m, s], recv_sem=recv.at[m, s],
            device_id=peer, device_id_type=pl.DeviceIdType.MESH)

    started = []

    def go(copy):
        copy.start()
        started.append(copy)
        return copy

    piece = rows // PIECES
    own = {}

    def embed(m):
        p = jnp.dot(features[m][...], w[m], preferred_element_type=jnp.float32)
        i = lax.rsqrt(jnp.sum(p * p, axis=1, keepdims=True) + norm_eps)
        proj[m] = p
        inv[m] = i
        emb[m, narrow] = (p * i).astype(jnp.bfloat16)

    def send_own(m):
        for k in range(PIECES):
            ref = emb.at[m, narrow, pl.ds(k * piece, piece)]
            own[m, 0, k] = go(remote(ref, ref, m, OWN_CORE + k, core_peer))
            own[m, 1, k] = go(remote(ref, ref, m, OWN_CHIP + k, chip_peer))

    def forward(m):
        for k in range(PIECES):
            own[m, 1, k].wait_recv()
            ref = emb.at[m, block_chip, pl.ds(k * piece, piece)]
            own[m, 2, k] = go(remote(ref, ref, m, FORWARD + k, core_peer))

    def arrived(m, kind):
        for k in range(PIECES):
            own[m, kind, k].wait_recv()

    loads[0].wait()
    embed(1)
    pl.semaphore_wait(barrier, len(peers))
    send_own(1)
    pairs[narrow] = partner[...]
    pair_copies = []
    for s, peer in enumerate((core_peer, chip_peer, far_peer)):
        copy = pltpu.make_async_remote_copy(
            src_ref=pairs.at[narrow], dst_ref=pairs.at[narrow], send_sem=p_send.at[s], recv_sem=p_recv.at[s],
            device_id=peer, device_id_type=pl.DeviceIdType.MESH)
        pair_copies.append(go(copy))
    loads[1].wait()
    embed(0)
    send_own(0)

    for m in (0, 1):
        ft[m] = features[m][...].T

    down = lax.broadcasted_iota(jnp.int32, (rows, rows), 0)
    along = lax.broadcasted_iota(jnp.int32, (rows, rows), 1)
    partner_down = jnp.sum(
        jnp.where(down == along, partner[...].astype(jnp.float32), 0.0), axis=1, keepdims=True
    ).astype(jnp.int32)

    def add_block(m, block, first):
        other = emb[1 - m, block]
        logits = logit_scale * lax.dot_general(
            emb[m, narrow], other, (((1,), (1,)), ((), ())), preferred_element_type=jnp.float32
        ) + logit_bias
        if m == 0:
            match = partner_down == block * rows + along
        else:
            match = pairs[block] == narrow * rows + down
        pair = jnp.where(match, -logit_scale, logit_scale) * jax.nn.sigmoid(jnp.where(match, -logits, logits))
        part = jnp.dot(pair.astype(jnp.bfloat16), other, preferred_element_type=jnp.float32)
        grad[m] = part if first else grad[m] + part

    def project_back(m):
        p, i, g = proj[m], inv[m], grad[m]
        total = jnp.sum(p * g, axis=1, keepdims=True)
        value = i * g - p * (i * i * i * total)
        pg[m] = value.astype(jnp.bfloat16)
        q = quarter
        moved = jnp.concatenate([value[:, :q], value[:, 2 * q:3 * q], value[:, q:2 * q], value[:, 3 * q:]], axis=1)
        pgp[m] = moved.astype(jnp.bfloat16)

    def feature_grad(m, out):
        out[...] = lax.dot_general(
            pg[m], w[m], (((1,), (1,)), ((), ())), preferred_element_type=jnp.float32
        ).astype(jnp.bfloat16)

    def share(m, xd, core):
        left = ft[m, pl.ds(pl.multiple_of(xd * chunk, 16), chunk), :]
        right = pgp[m, :, pl.ds(pl.multiple_of(core * CORE_STEP, 128), WINDOW)]
        return jnp.dot(left, right, preferred_element_type=jnp.float32)

    core_copies, z_copies = {}, {}

    def core_start(m):
        for k, xd in enumerate(x_targets):
            core_out[m, k] = share(m, xd, 1 - c).astype(jnp.bfloat16)
            core_copies[m, k] = go(remote(core_out.at[m, k], core_in.at[m, k], m, CORE_SUM + k, core_peer))

    def chip_share(m, k):
        total = share(m, x_targets[k], c)
        core_copies[m, k].wait_recv()
        acc[m, k] = total + core_in[m, k].astype(jnp.float32)

    class Ring:
        def __init__(self, n, pair, value):
            self.n, self.pair, self.value, self.copies = n, pair, value, {}

        def push(self, h, kind, peer, value):
            out, into = ring_bufs[self.n][h]
            out[kind] = value.astype(jnp.bfloat16)
            s = h * 3 + kind
            self.copies[h, kind] = go(pltpu.make_async_remote_copy(
                src_ref=out.at[kind], dst_ref=into.at[kind],
                send_sem=ring_send.at[self.n, s], recv_sem=ring_recv.at[self.n, s],
                device_id=peer, device_id_type=pl.DeviceIdType.MESH))

        def pull(self, h, kind):
            self.copies[h, kind].wait_recv()
            return ring_bufs[self.n][h][1][kind].astype(jnp.float32)

        def relay(self, h):
            self.push(h, 0, self.pair[h], self.value(0, h))

        def direct(self, h):
            self.push(h, 1, self.pair[1 - h], self.value(2 - h, h))

        def both(self):
            for h in range(2):
                self.push(h, 2, self.pair[h], self.value(1 + h, h) + self.pull(h, 0))

        def total(self, h):
            return self.value(3, h) + self.pull(h, 1) + self.pull(h, 2)

    def x_first(m, low):
        return lambda k, h: acc[m, k, h * half + low:(h + 1) * half, :]

    def column_part(l):
        return pl.ds(pl.multiple_of(l * PART_STEP, 128), PART)

    def y_second(sums, cuts):
        def value(k, h):
            t = y_targets[k]
            return sums[t // 2, cuts[h]:cuts[h + 1], column_part(lax.rem(t, 2))]
        return value

    def y_first(k, h):
        t = y_targets[k]
        block = pl.ds(pl.multiple_of((t // 2) * half, 8), Y_FIRST)
        return acc[1, 2 * h:2 * h + 2, block, column_part(lax.rem(t, 2))]

    def x_second(k, h):
        n = Y_FIRST // 2
        return sums_y[k, h * n:(h + 1) * n, :]

    cuts_i, cuts_t = (0, 80, half), (0, 48, half - Y_FIRST)
    ring_ix = Ring(0, x_pair, x_first(0, 0))
    ring_iy = Ring(1, y_pair, y_second(sums_i, cuts_i))
    ring_tx = Ring(2, x_pair, x_first(1, Y_FIRST))
    ring_txy = Ring(3, y_pair, y_second(sums_t, cuts_t))
    ring_ty = Ring(4, y_pair, y_first)
    ring_tyx = Ring(5, x_pair, x_second)

    def begin(ring):
        ring.relay(0)
        ring.relay(1)
        ring.direct(1)
        ring.direct(0)

    spare = PART - quarter
    segments = quarter // spare
    rest = mine - TILE

    def z_start(m):
        total = last[m]
        offset = (quarter - PART_STEP) * (yl + 2 * c)
        total = pltpu.roll(total, lax.rem(PART - offset, PART), 1)
        row = lax.broadcasted_iota(jnp.int32, (nz * TILE, half), 0)
        column = lax.broadcasted_iota(jnp.int32, (nz * TILE, half), 1)
        which, within = row // TILE, lax.rem(row, TILE)

        def pick(chosen, source, value):
            spread = jnp.where(chosen & (column == which * mine + source), 1.0, 0.0).astype(jnp.bfloat16)
            return jnp.dot(spread, value.astype(jnp.bfloat16), preferred_element_type=jnp.float32)

        body = pick(within < TILE, within, total)
        tail = jnp.zeros_like(body)
        for s in range(segments):
            moved = pltpu.roll(total, quarter - s * spare, 1)
            chosen = (within < rest * segments) & (lax.rem(within, segments) == s)
            tail = tail + pick(chosen, TILE + within // segments, moved)
        lane = lax.broadcasted_iota(jnp.int32, body.shape, 1)
        packed = jnp.where(lane < quarter, body, tail).astype(jnp.bfloat16)
        for d in range(nz):
            z_out[m, d] = packed[d * TILE:(d + 1) * TILE]
        for s, (zd, peer) in enumerate(z_peers):
            z_copies[m, s] = go(remote(z_out.at[m, zd], z_in.at[m, s], m, Z_SUM + s, peer))

    def z_finish(m, out):
        total = z_out[m, z].astype(jnp.float32)
        for s in range(nz - 1):
            z_copies[m, s].wait_recv()
            total = total + z_in[m, s].astype(jnp.float32)
        out[:TILE, :] = total[:, :quarter]
        for r in range(rest):
            rows_of = [total[r * segments + s:r * segments + s + 1, quarter:] for s in range(segments)]
            out[TILE + r:TILE + r + 1, :] = jnp.concatenate(rows_of, axis=1)

    add = add_block
    add(0, narrow, True)
    pair_copies[0].wait_recv()
    add(1, narrow, True)
    arrived(1, 0)
    add(0, block_core, False)
    arrived(0, 0)
    add(1, block_core, False)

    forward(1)
    add(0, block_chip, False)
    arrived(1, 2)
    add(0, block_far, False)
    project_back(0)
    core_start(0)
    chip_share(0, 0)
    ring_ix.relay(0)
    ring_ix.relay(1)
    chip_share(0, 1)
    ring_ix.direct(1)
    chip_share(0, 2)
    ring_ix.direct(0)
    chip_share(0, 3)
    feature_grad(0, fg_i)

    forward(0)
    pair_copies[1].wait_recv()
    pair_copies[2].wait_recv()
    add(1, block_chip, False)
    arrived(0, 2)
    add(1, block_far, False)
    project_back(1)
    core_start(1)
    ring_ix.both()
    chip_share(1, 0)
    ring_tx.relay(0)
    ring_tx.relay(1)
    chip_share(1, 1)
    ring_ty.relay(0)
    ring_ty.direct(0)
    ring_tx.direct(1)
    chip_share(1, 2)
    ring_tx.direct(0)
    chip_share(1, 3)
    ring_ty.relay(1)
    ring_ty.direct(1)

    for h in range(2):
        sums_i[h] = ring_ix.total(h)
    begin(ring_iy)
    ring_tx.both()
    ring_ty.both()
    ring_iy.both()
    feature_grad(1, fg_t)
    for h in range(2):
        sums_t[h] = ring_tx.total(h)
    begin(ring_txy)
    for h in range(2):
        sums_y[2 * h:2 * h + 2] = ring_ty.total(h)
    begin(ring_tyx)
    for h in range(2):
        last[0, cuts_i[h]:cuts_i[h + 1]] = ring_iy.total(h)
    z_start(0)
    ring_txy.both()
    ring_tyx.both()
    for h in range(2):
        n = Y_FIRST // 2
        last[1, h * n:(h + 1) * n] = ring_tyx.total(h)
    for h in range(2):
        last[1, Y_FIRST + cuts_t[h]:Y_FIRST + cuts_t[h + 1]] = ring_txy.total(h)
    z_start(1)
    z_finish(0, wg_i)
    z_finish(1, wg_t)
    for copy in started:
        copy.wait_send()


def hand_over(a, b, c, d, a_out, b_out, c_out, d_out):
    a_out[...], b_out[...], c_out[...], d_out[...] = a[...], b[...], c[...], d[...]


def local(nz, image_features, text_features, image_weight, text_weight, partner):
    rows, depth = image_features.shape
    width = image_weight.shape[1]
    chunk = depth // NX
    half = chunk // NYH
    mine = half // nz
    b16, f32 = jnp.bfloat16, jnp.float32
    vmem = pl.BlockSpec(memory_space=pltpu.VMEM)
    hbm = pl.BlockSpec(memory_space=pl.ANY)
    copies = Z_SUM + nz - 1
    rest = half - Y_FIRST
    ring_shapes = [
        ((half, WINDOW), (half, WINDOW)),
        ((80, PART), (half - 80, PART)),
        ((rest, WINDOW), (rest, WINDOW)),
        ((48, PART), (rest - 48, PART)),
        ((2, Y_FIRST, PART), (2, Y_FIRST, PART)),
        ((Y_FIRST // 2, PART), (Y_FIRST // 2, PART)),
    ]
    rings = [[[pltpu.VMEM((3, *shape), b16) for _ in range(2)] for shape in pair] for pair in ring_shapes]
    outs = pl.pallas_call(
        functools.partial(kernel, nz),
        out_shape=(
            jax.ShapeDtypeStruct((rows, depth), b16),
            jax.ShapeDtypeStruct((rows, depth), b16),
            jax.ShapeDtypeStruct((mine, width // 4), f32),
            jax.ShapeDtypeStruct((mine, width // 4), f32),
        ),
        in_specs=[vmem, vmem, hbm, hbm, vmem],
        out_specs=(vmem,) * 4,
        scratch_shapes=[
            pltpu.VMEM((2, depth, width), b16),
            pltpu.VMEM((2, depth, rows), b16),
            pltpu.VMEM((2, rows, width), f32),
            pltpu.VMEM((2, rows, 1), f32),
            pltpu.VMEM((2, rows, width), f32),
            pltpu.VMEM((2, 4, rows, width), b16),
            pltpu.VMEM((4, 1, rows), jnp.int32),
            pltpu.VMEM((2, rows, width), b16),
            pltpu.VMEM((2, rows, width), b16),
            pltpu.VMEM((2, 4, chunk, WINDOW), b16),
            pltpu.VMEM((2, 4, chunk, WINDOW), b16),
            pltpu.VMEM((2, 4, chunk, WINDOW), f32),
            pltpu.VMEM((2, half, WINDOW), f32),
            pltpu.VMEM((2, rest, WINDOW), f32),
            pltpu.VMEM((4, Y_FIRST, PART), f32),
            pltpu.VMEM((2, half, PART), f32),
            pltpu.VMEM((2, nz, TILE, PART), b16),
            pltpu.VMEM((2, nz - 1, TILE, PART), b16),
            rings,
            pltpu.SemaphoreType.DMA((2,)),
            pltpu.SemaphoreType.DMA((3,)),
            pltpu.SemaphoreType.DMA((3,)),
            pltpu.SemaphoreType.DMA((2, copies)),
            pltpu.SemaphoreType.DMA((2, copies)),
            pltpu.SemaphoreType.DMA((RINGS, 6)),
            pltpu.SemaphoreType.DMA((RINGS, 6)),
        ],
        compiler_params=pltpu.CompilerParams(
            collective_id=0, has_side_effects=True, vmem_limit_bytes=56 * 1024 * 1024),
        cost_estimate=pl.CostEstimate(flops=4_500_000_000, bytes_accessed=8_000_000, transcendentals=300_000),
    )(image_features, text_features, image_weight, text_weight, partner)
    return pl.pallas_call(
        hand_over,
        out_shape=[jax.ShapeDtypeStruct(out.shape, out.dtype) for out in outs],
        in_specs=[vmem] * 4,
        out_specs=[vmem] * 4,
    )(*outs)


def solution(mesh):
    in_specs = (
        P(("wide", "narrow"), None),
        P(("wide", "narrow"), None),
        P(),
        P(),
        P("wide", "narrow"),
    )
    out_specs = (
        P(("wide", "narrow"), None),
        P(("wide", "narrow"), None),
        P("wide", "narrow"),
        P("wide", "narrow"),
    )
    nz = mesh.shape["wide"] // (NX * NYH)
    return jax.shard_map(
        functools.partial(local, nz), mesh=mesh, in_specs=in_specs, out_specs=out_specs, check_vma=False)
```

```python
import functools

import jax
import jax.numpy as jnp
from jax import lax
from jax.experimental import pallas as pl
from jax.experimental.pallas import tpu as pltpu
from jax.sharding import PartitionSpec as P

logit_scale = 10.0
logit_bias = -2.0
norm_eps = 1e-06

NX, NYH = 4, 2
PIECES = 2
WINDOW = 640
CORE_STEP = 512
PART = 384
PART_STEP = 256
TILE = 16
PAD = 32
CUT = 80
Y_FIRST = 64

OWN_CORE, OWN_CHIP, FORWARD = 0, PIECES, 2 * PIECES
CORE_SUM = 3 * PIECES
Z_SUM = CORE_SUM + 8
RINGS = 6


Z_ORDER = (4, 3, -3, 2, -2, 1, -1, 0)


def kernel(nz, f_i, f_t, w_i_hbm, w_t_hbm, partner, fg_i, fg_t, wg_i, wg_t,
           w, ft, ft_z, proj, inv, grad, emb, pairs, pg, pgp,
           out_i, in_i, out_t, in_t, acc_i, acc, sums_i, sums_ix, sums_t, sums_y, last_i, last, z_out, z_in,
           long_bufs, ring_bufs, w_sem, p_send, p_recv, send, recv, long_send, long_recv, ring_send, ring_recv):
    rows, depth = f_i.shape
    width = w.shape[2]
    chunk = depth // NX
    half = chunk // NYH
    mine = half // nz
    quarter = width // 4
    features = (f_i, f_t)
    wide, narrow = lax.axis_index("wide"), lax.axis_index("narrow")
    z, yh, x = lax.rem(wide, nz), lax.rem(wide // nz, NYH), wide // (nz * NYH)
    yl, c = narrow // 2, lax.rem(narrow, 2)

    def device(x=x, yh=yh, z=z, yl=yl, c=c):
        return ((x * NYH + yh) * nz + z, yl * 2 + c)

    core_peer = device(c=1 - c)
    chip_peer = device(yl=1 - yl)
    far_peer = device(yl=1 - yl, c=1 - c)
    block_core, block_chip, block_far = yl * 2 + 1 - c, (1 - yl) * 2 + c, (1 - yl) * 2 + 1 - c
    x_next, x_prev, x_far = lax.rem(x + 1, NX), lax.rem(x + NX - 1, NX), lax.rem(x + 2, NX)
    y = yh * 2 + yl
    y_far, y_next, y_prev = lax.rem(y + 2, 4), lax.rem(y + 1, 4), lax.rem(y + 3, 4)
    x_targets = (x_far, x_next, x_prev, x)
    y_targets = (y_far, y_next, y_prev, y)
    x_pair = (device(x=x_next), device(x=x_prev))
    y_pair = tuple(device(yh=t // 2, yl=lax.rem(t, 2)) for t in (y_next, y_prev))
    z_peers = [(lax.rem(z + d, nz), device(z=lax.rem(z + d, nz))) for d in range(1, nz)]

    loads = []
    for m, src in ((1, w_t_hbm), (0, w_i_hbm)):
        load = pltpu.make_async_copy(src, w.at[m], w_sem.at[m])
        load.start()
        loads.append(load)

    barrier = pltpu.get_barrier_semaphore()
    peers = [core_peer, chip_peer, far_peer, *x_pair, device(yh=1 - yh, yl=1 - yl)]
    peers += [peer for _, peer in z_peers]
    for peer in peers:
        pl.semaphore_signal(barrier, inc=1, device_id=peer, device_id_type=pl.DeviceIdType.MESH)

    def remote(src, dst, m, s, peer):
        return pltpu.make_async_remote_copy(
            src_ref=src, dst_ref=dst, send_sem=send.at[m, s], recv_sem=recv.at[m, s],
            device_id=peer, device_id_type=pl.DeviceIdType.MESH)

    started = []

    def go(copy):
        copy.start()
        started.append(copy)
        return copy

    piece = rows // PIECES
    own = {}

    def embed(m):
        p = jnp.dot(features[m][...], w[m], preferred_element_type=jnp.float32)
        i = lax.rsqrt(jnp.sum(p * p, axis=1, keepdims=True) + norm_eps)
        proj[m] = p
        inv[m] = i
        emb[m, narrow] = (p * i).astype(jnp.bfloat16)

    def send_own(m):
        for k in range(PIECES):
            ref = emb.at[m, narrow, pl.ds(k * piece, piece)]
            own[m, 0, k] = go(remote(ref, ref, m, OWN_CORE + k, core_peer))
            own[m, 1, k] = go(remote(ref, ref, m, OWN_CHIP + k, chip_peer))

    def forward(m, k):
        own[m, 1, k].wait_recv()
        ref = emb.at[m, block_chip, pl.ds(k * piece, piece)]
        own[m, 2, k] = go(remote(ref, ref, m, FORWARD + k, core_peer))

    def arrived(m, kind):
        for k in range(PIECES):
            own[m, kind, k].wait_recv()

    loads[0].wait()
    embed(1)
    pl.semaphore_wait(barrier, len(peers))
    send_own(1)
    pairs[narrow] = partner[...]
    pair_copies = []
    for s, peer in enumerate((core_peer, chip_peer, far_peer)):
        copy = pltpu.make_async_remote_copy(
            src_ref=pairs.at[narrow], dst_ref=pairs.at[narrow], send_sem=p_send.at[s], recv_sem=p_recv.at[s],
            device_id=peer, device_id_type=pl.DeviceIdType.MESH)
        pair_copies.append(go(copy))
    loads[1].wait()
    embed(0)
    send_own(0)

    ft[...] = f_t[...].T
    row = lax.broadcasted_iota(jnp.int32, (half, 1), 0)
    source = (row // mine) * half + lax.rem(row, mine)
    column = lax.broadcasted_iota(jnp.int32, (half, depth), 1)
    for d in range(nz):
        order = jnp.where(column == source + d * mine, 1.0, 0.0).astype(jnp.bfloat16)
        ft_z[d] = lax.dot_general(
            order, f_i[...], (((1,), (1,)), ((), ())), preferred_element_type=jnp.float32
        ).astype(jnp.bfloat16)

    down = lax.broadcasted_iota(jnp.int32, (rows, rows), 0)
    along = lax.broadcasted_iota(jnp.int32, (rows, rows), 1)
    partner_down = jnp.sum(
        jnp.where(down == along, partner[...].astype(jnp.float32), 0.0), axis=1, keepdims=True
    ).astype(jnp.int32)

    def add_block(m, block, first):
        other = emb[1 - m, block]
        logits = logit_scale * lax.dot_general(
            emb[m, narrow], other, (((1,), (1,)), ((), ())), preferred_element_type=jnp.float32
        ) + logit_bias
        if m == 0:
            match = partner_down == block * rows + along
        else:
            match = pairs[block] == narrow * rows + down
        pair = jnp.where(match, -logit_scale, logit_scale) * jax.nn.sigmoid(jnp.where(match, -logits, logits))
        part = jnp.dot(pair.astype(jnp.bfloat16), other, preferred_element_type=jnp.float32)
        grad[m] = part if first else grad[m] + part

    def project_back(m):
        p, i, g = proj[m], inv[m], grad[m]
        total = jnp.sum(p * g, axis=1, keepdims=True)
        value = i * g - p * (i * i * i * total)
        pg[m] = value.astype(jnp.bfloat16)
        q = quarter
        moved = jnp.concatenate([value[:, :q], value[:, 2 * q:3 * q], value[:, q:2 * q], value[:, 3 * q:]], axis=1)
        pgp[m] = moved.astype(jnp.bfloat16)

    def feature_grad(m, out):
        out[...] = lax.dot_general(
            pg[m], w[m], (((1,), (1,)), ((), ())), preferred_element_type=jnp.float32
        ).astype(jnp.bfloat16)

    def share(left, m, core):
        right = pgp[m, :, pl.ds(pl.multiple_of(core * CORE_STEP, 128), WINDOW)]
        return jnp.dot(left, right, preferred_element_type=jnp.float32)

    def rows_of(m, k):
        if m == 0:
            return ft_z[lax.rem(z + Z_ORDER[k] + nz, nz)]
        return ft[pl.ds(pl.multiple_of(x_targets[k] * chunk, 16), chunk), :]

    core_copies, z_copies = {}, {}
    core_bufs = ((out_i, in_i, acc_i), (out_t, in_t, acc))

    def core_start(m, k):
        out, into, _ = core_bufs[m]
        out[k] = share(rows_of(m, k), m, 1 - c).astype(jnp.bfloat16)
        core_copies[m, k] = go(remote(out.at[k], into.at[k], m, CORE_SUM + k, core_peer))

    def chip_share(m, k):
        _, into, total = core_bufs[m]
        part = share(rows_of(m, k), m, c)
        core_copies[m, k].wait_recv()
        total[k] = part + into[k].astype(jnp.float32)

    z_pair = (device(z=lax.rem(z + 1, nz)), device(z=lax.rem(z + nz - 1, nz)))
    spans = (pl.ds(0, CUT), pl.ds(CUT, half - CUT))
    long_copies = {}

    def own_part(d, h):
        return acc_i[Z_ORDER.index(d), spans[h], :]

    def long_push(way, hops, far):
        h = way if far else 1 - way
        out, into = long_bufs[way][h]
        value = own_part(hops if way == 0 or hops == nz // 2 else -hops, h)
        first = nz // 2 if far else nz // 2 - 1
        if hops < first:
            value = value + long_pull(way, hops + 1, far)
        slot = first - hops
        out[slot] = value.astype(jnp.bfloat16)
        s = 2 * slot + (0 if far else 1)
        long_copies[way, hops, far] = go(pltpu.make_async_remote_copy(
            src_ref=out.at[slot], dst_ref=into.at[slot], send_sem=long_send.at[way, s], recv_sem=long_recv.at[way, s],
            device_id=z_pair[way], device_id_type=pl.DeviceIdType.MESH))

    def long_pull(way, hops, far):
        long_copies[way, hops, far].wait_recv()
        h = way if far else 1 - way
        first = nz // 2 if far else nz // 2 - 1
        return long_bufs[way][h][1][first - hops].astype(jnp.float32)

    def long_step(hops, far):
        for way in range(2):
            long_push(way, hops, far)

    def spread_rows():
        low = own_part(0, 0) + long_pull(0, 1, True) + long_pull(1, 1, False)
        high = own_part(0, 1) + long_pull(0, 1, False) + long_pull(1, 1, True)
        row = lax.broadcasted_iota(jnp.int32, (8 * PAD, 1), 0)
        within = lax.rem(row, PAD)
        source = jnp.where(within < mine, (row // PAD) * mine + within, -1)
        column = lax.broadcasted_iota(jnp.int32, (8 * PAD, half), 1)
        spread = jnp.where(column == source, 1.0, 0.0).astype(jnp.bfloat16)
        total = jnp.concatenate([low, high], axis=0).astype(jnp.bfloat16)
        total = jnp.dot(spread, total, preferred_element_type=jnp.float32)
        for d in range(8):
            sums_i[d] = total[d * PAD:(d + 1) * PAD]

    class Ring:
        def __init__(self, n, pair, value):
            self.n, self.pair, self.value, self.copies = n, pair, value, {}

        def push(self, h, kind, peer, value):
            out, into = ring_bufs[self.n][h]
            out[kind] = value.astype(jnp.bfloat16)
            s = h * 3 + kind
            self.copies[h, kind] = go(pltpu.make_async_remote_copy(
                src_ref=out.at[kind], dst_ref=into.at[kind],
                send_sem=ring_send.at[self.n, s], recv_sem=ring_recv.at[self.n, s],
                device_id=peer, device_id_type=pl.DeviceIdType.MESH))

        def pull(self, h, kind):
            self.copies[h, kind].wait_recv()
            return ring_bufs[self.n][h][1][kind].astype(jnp.float32)

        def relay(self, h):
            self.push(h, 0, self.pair[h], self.value(0, h))

        def direct(self, h):
            self.push(h, 1, self.pair[1 - h], self.value(2 - h, h))

        def both(self):
            for h in range(2):
                self.push(h, 2, self.pair[h], self.value(1 + h, h) + self.pull(h, 0))

        def total(self, h):
            return self.value(3, h) + self.pull(h, 1) + self.pull(h, 2)

    def x_first(k, h):
        return acc[k, h * half + Y_FIRST:(h + 1) * half, :]

    def x_after_z(k, h):
        return sums_i[x_targets[k] * NYH + h]

    def column_part(l):
        return pl.ds(pl.multiple_of(l * PART_STEP, 128), PART)

    def y_second(sums, cuts):
        def value(k, h):
            t = y_targets[k]
            return sums[t // 2, cuts[h]:cuts[h + 1], column_part(lax.rem(t, 2))]
        return value

    def y_first(k, h):
        t = y_targets[k]
        block = pl.ds(pl.multiple_of((t // 2) * half, 8), Y_FIRST)
        return acc[2 * h:2 * h + 2, block, column_part(lax.rem(t, 2))]

    def x_second(k, h):
        n = Y_FIRST // 2
        return sums_y[k, h * n:(h + 1) * n, :]

    cuts_i, cuts_t = (0, PAD // 2, PAD), (0, 48, half - Y_FIRST)
    ring_ix = Ring(0, x_pair, x_after_z)
    ring_iy = Ring(1, y_pair, y_second(sums_ix, cuts_i))
    ring_tx = Ring(2, x_pair, x_first)
    ring_txy = Ring(3, y_pair, y_second(sums_t, cuts_t))
    ring_ty = Ring(4, y_pair, y_first)
    ring_tyx = Ring(5, x_pair, x_second)

    def begin(ring):
        ring.relay(0)
        ring.relay(1)
        ring.direct(1)
        ring.direct(0)

    spare = PART - quarter
    segments = quarter // spare
    rest = mine - TILE

    def to_left(value):
        offset = (quarter - PART_STEP) * (yl + 2 * c)
        return pltpu.roll(value, lax.rem(PART - offset, PART), 1)

    def z_start():
        total = to_left(last[...])
        row = lax.broadcasted_iota(jnp.int32, (nz * TILE, half), 0)
        column = lax.broadcasted_iota(jnp.int32, (nz * TILE, half), 1)
        which, within = row // TILE, lax.rem(row, TILE)

        def pick(chosen, source, value):
            spread = jnp.where(chosen & (column == which * mine + source), 1.0, 0.0).astype(jnp.bfloat16)
            return jnp.dot(spread, value.astype(jnp.bfloat16), preferred_element_type=jnp.float32)

        body = pick(within < TILE, within, total)
        tail = jnp.zeros_like(body)
        for s in range(segments):
            moved = pltpu.roll(total, quarter - s * spare, 1)
            chosen = (within < rest * segments) & (lax.rem(within, segments) == s)
            tail = tail + pick(chosen, TILE + within // segments, moved)
        lane = lax.broadcasted_iota(jnp.int32, body.shape, 1)
        packed = jnp.where(lane < quarter, body, tail).astype(jnp.bfloat16)
        for d in range(nz):
            z_out[d] = packed[d * TILE:(d + 1) * TILE]
        for s, (zd, peer) in enumerate(z_peers):
            z_copies[s] = go(remote(z_out.at[zd], z_in.at[s], 1, Z_SUM + s, peer))

    def z_finish(out):
        total = z_out[z].astype(jnp.float32)
        for s in range(nz - 1):
            z_copies[s].wait_recv()
            total = total + z_in[s].astype(jnp.float32)
        out[:TILE, :] = total[:, :quarter]
        for r in range(rest):
            pieces = [total[r * segments + s:r * segments + s + 1, quarter:] for s in range(segments)]
            out[TILE + r:TILE + r + 1, :] = jnp.concatenate(pieces, axis=1)

    add = add_block
    add(0, narrow, True)
    pair_copies[0].wait_recv()
    add(1, narrow, True)
    arrived(1, 0)
    add(0, block_core, False)
    arrived(0, 0)
    add(1, block_core, False)

    forward(1, 0)
    forward(1, 1)
    add(0, block_chip, False)
    arrived(1, 2)
    add(0, block_far, False)
    project_back(0)
    half_z = nz // 2
    ahead = 3
    for k in range(nz + ahead):
        if k < nz:
            core_start(0, k)
        if k == ahead:
            chip_share(0, 0)
            long_step(half_z, True)
        elif k == ahead + 1 or k == ahead + 2:
            chip_share(0, k - ahead)
            long_push(k - ahead - 1, half_z - 1, False)
        elif k > ahead:
            chip_share(0, k - ahead)
    forward(0, 0)
    feature_grad(0, fg_i)
    long_step(3, True)

    forward(0, 1)
    pair_copies[1].wait_recv()
    pair_copies[2].wait_recv()
    add(1, block_chip, False)
    arrived(0, 2)
    add(1, block_far, False)
    project_back(1)
    core_start(1, 0)
    core_start(1, 1)
    core_start(1, 2)
    chip_share(1, 0)
    ring_tx.relay(0)
    ring_tx.relay(1)
    core_start(1, 3)
    chip_share(1, 1)
    ring_ty.relay(0)
    ring_ty.direct(0)
    ring_tx.direct(1)
    chip_share(1, 2)
    ring_tx.direct(0)
    chip_share(1, 3)
    ring_ty.relay(1)
    ring_ty.direct(1)
    long_step(2, False)
    long_step(2, True)

    ring_tx.both()
    ring_ty.both()
    long_step(1, False)
    long_step(1, True)
    feature_grad(1, fg_t)
    for h in range(2):
        sums_t[h] = ring_tx.total(h)
    begin(ring_txy)
    for h in range(2):
        sums_y[2 * h:2 * h + 2] = ring_ty.total(h)
    begin(ring_tyx)
    spread_rows()
    begin(ring_ix)
    ring_txy.both()
    ring_tyx.both()
    ring_ix.both()
    for h in range(2):
        n = Y_FIRST // 2
        last[h * n:(h + 1) * n] = ring_tyx.total(h)
    for h in range(2):
        last[Y_FIRST + cuts_t[h]:Y_FIRST + cuts_t[h + 1]] = ring_txy.total(h)
    z_start()
    for h in range(2):
        sums_ix[h] = ring_ix.total(h)
    begin(ring_iy)
    ring_iy.both()
    for h in range(2):
        last_i[cuts_i[h]:cuts_i[h + 1]] = ring_iy.total(h)
    wg_i[...] = to_left(last_i[...])[:mine, :quarter]
    z_finish(wg_t)
    for copy in started:
        copy.wait_send()


def hand_over(a, b, c, d, a_out, b_out, c_out, d_out):
    a_out[...], b_out[...], c_out[...], d_out[...] = a[...], b[...], c[...], d[...]


def local(nz, image_features, text_features, image_weight, text_weight, partner):
    rows, depth = image_features.shape
    width = image_weight.shape[1]
    chunk = depth // NX
    half = chunk // NYH
    mine = half // nz
    b16, f32 = jnp.bfloat16, jnp.float32
    vmem = pl.BlockSpec(memory_space=pltpu.VMEM)
    hbm = pl.BlockSpec(memory_space=pl.ANY)
    copies = Z_SUM + nz - 1
    rest = half - Y_FIRST
    ring_shapes = [
        ((PAD, WINDOW), (PAD, WINDOW)),
        ((PAD // 2, PART), (PAD // 2, PART)),
        ((rest, WINDOW), (rest, WINDOW)),
        ((48, PART), (rest - 48, PART)),
        ((2, Y_FIRST, PART), (2, Y_FIRST, PART)),
        ((Y_FIRST // 2, PART), (Y_FIRST // 2, PART)),
    ]
    rings = [[[pltpu.VMEM((3, *shape), b16) for _ in range(2)] for shape in pair] for pair in ring_shapes]
    long_rows, hops = (CUT, half - CUT), nz // 2
    longs = [
        [[pltpu.VMEM((hops if h == way else hops - 1, long_rows[h], WINDOW), b16) for _ in range(2)] for h in range(2)]
        for way in range(2)
    ]
    outs = pl.pallas_call(
        functools.partial(kernel, nz),
        out_shape=(
            jax.ShapeDtypeStruct((rows, depth), b16),
            jax.ShapeDtypeStruct((rows, depth), b16),
            jax.ShapeDtypeStruct((mine, width // 4), f32),
            jax.ShapeDtypeStruct((mine, width // 4), f32),
        ),
        in_specs=[vmem, vmem, hbm, hbm, vmem],
        out_specs=(vmem,) * 4,
        scratch_shapes=[
            pltpu.VMEM((2, depth, width), b16),
            pltpu.VMEM((depth, rows), b16),
            pltpu.VMEM((nz, half, rows), b16),
            pltpu.VMEM((2, rows, width), f32),
            pltpu.VMEM((2, rows, 1), f32),
            pltpu.VMEM((2, rows, width), f32),
            pltpu.VMEM((2, 4, rows, width), b16),
            pltpu.VMEM((4, 1, rows), jnp.int32),
            pltpu.VMEM((2, rows, width), b16),
            pltpu.VMEM((2, rows, width), b16),
            pltpu.VMEM((nz, half, WINDOW), b16),
            pltpu.VMEM((nz, half, WINDOW), b16),
            pltpu.VMEM((4, chunk, WINDOW), b16),
            pltpu.VMEM((4, chunk, WINDOW), b16),
            pltpu.VMEM((nz, half, WINDOW), f32),
            pltpu.VMEM((4, chunk, WINDOW), f32),
            pltpu.VMEM((8, PAD, WINDOW), f32),
            pltpu.VMEM((2, PAD, WINDOW), f32),
            pltpu.VMEM((2, rest, WINDOW), f32),
            pltpu.VMEM((4, Y_FIRST, PART), f32),
            pltpu.VMEM((PAD, PART), f32),
            pltpu.VMEM((half, PART), f32),
            pltpu.VMEM((nz, TILE, PART), b16),
            pltpu.VMEM((nz - 1, TILE, PART), b16),
            longs,
            rings,
            pltpu.SemaphoreType.DMA((2,)),
            pltpu.SemaphoreType.DMA((3,)),
            pltpu.SemaphoreType.DMA((3,)),
            pltpu.SemaphoreType.DMA((2, copies)),
            pltpu.SemaphoreType.DMA((2, copies)),
            pltpu.SemaphoreType.DMA((2, 7)),
            pltpu.SemaphoreType.DMA((2, 7)),
            pltpu.SemaphoreType.DMA((RINGS, 6)),
            pltpu.SemaphoreType.DMA((RINGS, 6)),
        ],
        compiler_params=pltpu.CompilerParams(
            collective_id=0, has_side_effects=True, vmem_limit_bytes=56 * 1024 * 1024),
        cost_estimate=pl.CostEstimate(flops=4_500_000_000, bytes_accessed=8_000_000, transcendentals=300_000),
    )(image_features, text_features, image_weight, text_weight, partner)
    return pl.pallas_call(
        hand_over,
        out_shape=[jax.ShapeDtypeStruct(out.shape, out.dtype) for out in outs],
        in_specs=[vmem] * 4,
        out_specs=[vmem] * 4,
    )(*outs)


def solution(mesh):
    in_specs = (
        P(("wide", "narrow"), None),
        P(("wide", "narrow"), None),
        P(),
        P(),
        P("wide", "narrow"),
    )
    out_specs = (
        P(("wide", "narrow"), None),
        P(("wide", "narrow"), None),
        P("wide", "narrow"),
        P("wide", "narrow"),
    )
    nz = mesh.shape["wide"] // (NX * NYH)
    return jax.shard_map(
        functools.partial(local, nz), mesh=mesh, in_specs=in_specs, out_specs=out_specs, check_vma=False)
```

```python
import functools

import jax
import jax.numpy as jnp
from jax import lax
from jax.experimental import pallas as pl
from jax.experimental.pallas import tpu as pltpu
from jax.sharding import PartitionSpec as P

logit_scale = 10.0
logit_bias = -2.0
norm_eps = 1e-06

NX, NYH = 4, 2
PIECES = 2
WINDOW = 640
CORE_STEP = 512
PART = 384
PART_STEP = 256
TILE = 16
Y_FIRST = 64

OWN_CORE, OWN_CHIP, FORWARD = 0, PIECES, 2 * PIECES
CORE_SUM = 3 * PIECES
Z_SUM = CORE_SUM + 4
RINGS = 6


def kernel(nz, f_i_hbm, f_t_hbm, w_i_hbm, w_t_hbm, partner_hbm, fg_i_hbm, fg_t_hbm, wg_i, wg_t,
           f_i, f_t, partner, fg, fg_sem, w, ft, proj, inv, grad, emb, pairs, pg, pgp,
           core_out, core_in, acc, sums_i, sums_t, sums_y, last, z_out, z_in, ring_bufs,
           f_sem, w_sem, p_send, p_recv, send, recv, ring_send, ring_recv):
    rows, depth = f_i.shape
    width = w.shape[2]
    chunk = depth // NX
    half = chunk // NYH
    mine = half // nz
    quarter = width // 4
    features = (f_i, f_t)
    wide, narrow = lax.axis_index("wide"), lax.axis_index("narrow")
    z, yh, x = lax.rem(wide, nz), lax.rem(wide // nz, NYH), wide // (nz * NYH)
    yl, c = narrow // 2, lax.rem(narrow, 2)

    def device(x=x, yh=yh, z=z, yl=yl, c=c):
        return ((x * NYH + yh) * nz + z, yl * 2 + c)

    core_peer = device(c=1 - c)
    chip_peer = device(yl=1 - yl)
    far_peer = device(yl=1 - yl, c=1 - c)
    block_core, block_chip, block_far = yl * 2 + 1 - c, (1 - yl) * 2 + c, (1 - yl) * 2 + 1 - c
    x_next, x_prev, x_far = lax.rem(x + 1, NX), lax.rem(x + NX - 1, NX), lax.rem(x + 2, NX)
    y = yh * 2 + yl
    y_far, y_next, y_prev = lax.rem(y + 2, 4), lax.rem(y + 1, 4), lax.rem(y + 3, 4)
    x_targets = (x_far, x_next, x_prev, x)
    y_targets = (y_far, y_next, y_prev, y)
    x_pair = (device(x=x_next), device(x=x_prev))
    y_pair = tuple(device(yh=t // 2, yl=lax.rem(t, 2)) for t in (y_next, y_prev))
    z_peers = [(lax.rem(z + d, nz), device(z=lax.rem(z + d, nz))) for d in range(1, nz)]

    barrier = pltpu.get_barrier_semaphore()
    peers = [core_peer, chip_peer, far_peer, *x_pair, device(yh=1 - yh, yl=1 - yl)]
    peers += [peer for _, peer in z_peers]
    for peer in peers:
        pl.semaphore_signal(barrier, inc=1, device_id=peer, device_id_type=pl.DeviceIdType.MESH)

    loads = []
    sources = ((f_t_hbm, f_t), (f_i_hbm, f_i), (partner_hbm, partner))
    feature_loads = [pltpu.make_async_copy(src, dst, f_sem.at[k]) for k, (src, dst) in enumerate(sources)]
    feature_loads[0].start()
    for m, src in ((1, w_t_hbm), (0, w_i_hbm)):
        load = pltpu.make_async_copy(src, w.at[m], w_sem.at[m])
        load.start()
        loads.append(load)
    feature_loads[1].start()
    feature_loads[2].start()

    def remote(src, dst, m, s, peer):
        return pltpu.make_async_remote_copy(
            src_ref=src, dst_ref=dst, send_sem=send.at[m, s], recv_sem=recv.at[m, s],
            device_id=peer, device_id_type=pl.DeviceIdType.MESH)

    started = []

    def go(copy):
        copy.start()
        started.append(copy)
        return copy

    piece = rows // PIECES
    own = {}

    def embed(m):
        p = jnp.dot(features[m][...], w[m], preferred_element_type=jnp.float32)
        i = lax.rsqrt(jnp.sum(p * p, axis=1, keepdims=True) + norm_eps)
        proj[m] = p
        inv[m] = i
        emb[m, narrow] = (p * i).astype(jnp.bfloat16)

    def send_own(m):
        for k in range(PIECES):
            ref = emb.at[m, narrow, pl.ds(k * piece, piece)]
            own[m, 0, k] = go(remote(ref, ref, m, OWN_CORE + k, core_peer))
            own[m, 1, k] = go(remote(ref, ref, m, OWN_CHIP + k, chip_peer))

    def forward(m):
        for k in range(PIECES):
            own[m, 1, k].wait_recv()
            ref = emb.at[m, block_chip, pl.ds(k * piece, piece)]
            own[m, 2, k] = go(remote(ref, ref, m, FORWARD + k, core_peer))

    def arrived(m, kind):
        for k in range(PIECES):
            own[m, kind, k].wait_recv()

    feature_loads[0].wait()
    loads[0].wait()
    embed(1)
    pl.semaphore_wait(barrier, len(peers))
    send_own(1)
    feature_loads[2].wait()
    pairs[narrow] = partner[...]
    pair_copies = []
    for s, peer in enumerate((core_peer, chip_peer, far_peer)):
        copy = pltpu.make_async_remote_copy(
            src_ref=pairs.at[narrow], dst_ref=pairs.at[narrow], send_sem=p_send.at[s], recv_sem=p_recv.at[s],
            device_id=peer, device_id_type=pl.DeviceIdType.MESH)
        pair_copies.append(go(copy))
    feature_loads[1].wait()
    loads[1].wait()
    embed(0)
    send_own(0)

    for m in (0, 1):
        ft[m] = features[m][...].T

    down = lax.broadcasted_iota(jnp.int32, (rows, rows), 0)
    along = lax.broadcasted_iota(jnp.int32, (rows, rows), 1)
    partner_down = jnp.sum(
        jnp.where(down == along, partner[...].astype(jnp.float32), 0.0), axis=1, keepdims=True
    ).astype(jnp.int32)

    def add_block(m, block, first):
        other = emb[1 - m, block]
        logits = logit_scale * lax.dot_general(
            emb[m, narrow], other, (((1,), (1,)), ((), ())), preferred_element_type=jnp.float32
        ) + logit_bias
        if m == 0:
            match = partner_down == block * rows + along
        else:
            match = pairs[block] == narrow * rows + down
        pair = jnp.where(match, -logit_scale, logit_scale) * jax.nn.sigmoid(jnp.where(match, -logits, logits))
        part = jnp.dot(pair.astype(jnp.bfloat16), other, preferred_element_type=jnp.float32)
        grad[m] = part if first else grad[m] + part

    def project_back(m):
        p, i, g = proj[m], inv[m], grad[m]
        total = jnp.sum(p * g, axis=1, keepdims=True)
        value = i * g - p * (i * i * i * total)
        value = value.astype(jnp.bfloat16)
        pg[m] = value
        q = quarter
        pgp[m] = jnp.concatenate([value[:, :q], value[:, 2 * q:3 * q], value[:, q:2 * q], value[:, 3 * q:]], axis=1)

    fg_copies = []

    def feature_grad(m, out):
        fg[m] = lax.dot_general(
            pg[m], w[m], (((1,), (1,)), ((), ())), preferred_element_type=jnp.float32
        ).astype(jnp.bfloat16)
        copy = pltpu.make_async_copy(fg.at[m], out, fg_sem.at[m])
        copy.start()
        fg_copies.append(copy)

    def share(m, xd, core):
        left = ft[m, pl.ds(pl.multiple_of(xd * chunk, 16), chunk), :]
        right = pgp[m, :, pl.ds(pl.multiple_of(core * CORE_STEP, 128), WINDOW)]
        return jnp.dot(left, right, preferred_element_type=jnp.float32)

    core_copies, z_copies = {}, {}

    def core_start(m, k):
        core_out[m, k] = share(m, x_targets[k], 1 - c).astype(jnp.bfloat16)
        core_copies[m, k] = go(remote(core_out.at[m, k], core_in.at[m, k], m, CORE_SUM + k, core_peer))

    def chip_share(m, k):
        total = share(m, x_targets[k], c)
        core_copies[m, k].wait_recv()
        acc[m, k] = total + core_in[m, k].astype(jnp.float32)

    class Ring:
        def __init__(self, n, pair, value):
            self.n, self.pair, self.value, self.copies = n, pair, value, {}

        def push(self, h, kind, peer, value):
            out, into = ring_bufs[self.n][h]
            out[kind] = value.astype(jnp.bfloat16)
            s = h * 3 + kind
            self.copies[h, kind] = go(pltpu.make_async_remote_copy(
                src_ref=out.at[kind], dst_ref=into.at[kind],
                send_sem=ring_send.at[self.n, s], recv_sem=ring_recv.at[self.n, s],
                device_id=peer, device_id_type=pl.DeviceIdType.MESH))

        def pull(self, h, kind):
            self.copies[h, kind].wait_recv()
            return ring_bufs[self.n][h][1][kind].astype(jnp.float32)

        def relay(self, h):
            self.push(h, 0, self.pair[h], self.value(0, h))

        def direct(self, h):
            self.push(h, 1, self.pair[1 - h], self.value(2 - h, h))

        def both(self):
            for h in range(2):
                self.push(h, 2, self.pair[h], self.value(1 + h, h) + self.pull(h, 0))

        def total(self, h):
            return self.value(3, h) + self.pull(h, 1) + self.pull(h, 2)

    def x_first(m, low):
        return lambda k, h: acc[m, k, h * half + low:(h + 1) * half, :]

    def column_part(l):
        return pl.ds(pl.multiple_of(l * PART_STEP, 128), PART)

    def y_second(sums, cuts):
        def value(k, h):
            t = y_targets[k]
            return sums[t // 2, cuts[h]:cuts[h + 1], column_part(lax.rem(t, 2))]
        return value

    def y_first(k, h):
        t = y_targets[k]
        block = pl.ds(pl.multiple_of((t // 2) * half, 8), Y_FIRST)
        return acc[1, 2 * h:2 * h + 2, block, column_part(lax.rem(t, 2))]

    def x_second(k, h):
        n = Y_FIRST // 2
        return sums_y[k, h * n:(h + 1) * n, :]

    cuts_i, cuts_t = (0, 80, half), (0, 48, half - Y_FIRST)
    ring_ix = Ring(0, x_pair, x_first(0, 0))
    ring_iy = Ring(1, y_pair, y_second(sums_i, cuts_i))
    ring_tx = Ring(2, x_pair, x_first(1, Y_FIRST))
    ring_txy = Ring(3, y_pair, y_second(sums_t, cuts_t))
    ring_ty = Ring(4, y_pair, y_first)
    ring_tyx = Ring(5, x_pair, x_second)

    def begin(ring):
        ring.relay(0)
        ring.relay(1)
        ring.direct(1)
        ring.direct(0)

    spare = PART - quarter
    segments = quarter // spare
    rest = mine - TILE

    def z_start(m):
        total = last[m]
        offset = (quarter - PART_STEP) * (yl + 2 * c)
        total = pltpu.roll(total, lax.rem(PART - offset, PART), 1)
        row = lax.broadcasted_iota(jnp.int32, (nz * TILE, half), 0)
        column = lax.broadcasted_iota(jnp.int32, (nz * TILE, half), 1)
        which, within = row // TILE, lax.rem(row, TILE)

        def pick(chosen, source, value):
            spread = jnp.where(chosen & (column == which * mine + source), 1.0, 0.0).astype(jnp.bfloat16)
            return jnp.dot(spread, value.astype(jnp.bfloat16), preferred_element_type=jnp.float32)

        body = pick(within < TILE, within, total)
        tail = jnp.zeros_like(body)
        for s in range(segments):
            moved = pltpu.roll(total, quarter - s * spare, 1)
            chosen = (within < rest * segments) & (lax.rem(within, segments) == s)
            tail = tail + pick(chosen, TILE + within // segments, moved)
        lane = lax.broadcasted_iota(jnp.int32, body.shape, 1)
        packed = jnp.where(lane < quarter, body, tail).astype(jnp.bfloat16)
        for d in range(nz):
            z_out[m, d] = packed[d * TILE:(d + 1) * TILE]
        for s, (zd, peer) in enumerate(z_peers):
            z_copies[m, s] = go(remote(z_out.at[m, zd], z_in.at[m, s], m, Z_SUM + s, peer))

    def z_finish(m, out):
        total = z_out[m, z].astype(jnp.float32)
        for s in range(nz - 1):
            z_copies[m, s].wait_recv()
            total = total + z_in[m, s].astype(jnp.float32)
        out[:TILE, :] = total[:, :quarter]
        for r in range(rest):
            rows_of = [total[r * segments + s:r * segments + s + 1, quarter:] for s in range(segments)]
            out[TILE + r:TILE + r + 1, :] = jnp.concatenate(rows_of, axis=1)

    add = add_block
    add(0, narrow, True)
    pair_copies[0].wait_recv()
    add(1, narrow, True)
    arrived(1, 0)
    add(0, block_core, False)
    arrived(0, 0)
    add(1, block_core, False)

    forward(1)
    add(0, block_chip, False)
    arrived(1, 2)
    add(0, block_far, False)
    project_back(0)
    core_start(0, 0)
    core_start(0, 1)
    core_start(0, 2)
    chip_share(0, 0)
    ring_ix.relay(0)
    ring_ix.relay(1)
    core_start(0, 3)
    chip_share(0, 1)
    ring_ix.direct(1)
    chip_share(0, 2)
    ring_ix.direct(0)
    chip_share(0, 3)
    feature_grad(0, fg_i_hbm)

    forward(0)
    pair_copies[1].wait_recv()
    pair_copies[2].wait_recv()
    add(1, block_chip, False)
    arrived(0, 2)
    add(1, block_far, False)
    project_back(1)
    core_start(1, 0)
    core_start(1, 1)
    core_start(1, 2)
    ring_ix.both()
    chip_share(1, 0)
    ring_tx.relay(0)
    ring_tx.relay(1)
    core_start(1, 3)
    chip_share(1, 1)
    ring_ty.relay(0)
    ring_ty.direct(0)
    ring_tx.direct(1)
    chip_share(1, 2)
    ring_tx.direct(0)
    chip_share(1, 3)
    ring_ty.relay(1)
    ring_ty.direct(1)

    for h in range(2):
        sums_i[h] = ring_ix.total(h)
    begin(ring_iy)
    ring_tx.both()
    ring_ty.both()
    ring_iy.both()
    feature_grad(1, fg_t_hbm)
    for h in range(2):
        sums_t[h] = ring_tx.total(h)
    begin(ring_txy)
    for h in range(2):
        sums_y[2 * h:2 * h + 2] = ring_ty.total(h)
    begin(ring_tyx)
    for h in range(2):
        last[0, cuts_i[h]:cuts_i[h + 1]] = ring_iy.total(h)
    z_start(0)
    ring_txy.both()
    ring_tyx.both()
    for h in range(2):
        n = Y_FIRST // 2
        last[1, h * n:(h + 1) * n] = ring_tyx.total(h)
    for h in range(2):
        last[1, Y_FIRST + cuts_t[h]:Y_FIRST + cuts_t[h + 1]] = ring_txy.total(h)
    z_start(1)
    z_finish(0, wg_i)
    z_finish(1, wg_t)
    for copy in fg_copies:
        copy.wait()
    for copy in started:
        copy.wait_send()


def hand_over(a, b, c, d, a_out, b_out, c_out, d_out):
    a_out[...], b_out[...], c_out[...], d_out[...] = a[...], b[...], c[...], d[...]


def local(nz, image_features, text_features, image_weight, text_weight, partner):
    rows, depth = image_features.shape
    width = image_weight.shape[1]
    chunk = depth // NX
    half = chunk // NYH
    mine = half // nz
    b16, f32 = jnp.bfloat16, jnp.float32
    vmem = pl.BlockSpec(memory_space=pltpu.VMEM)
    hbm = pl.BlockSpec(memory_space=pl.ANY)
    copies = Z_SUM + nz - 1
    rest = half - Y_FIRST
    ring_shapes = [
        ((half, WINDOW), (half, WINDOW)),
        ((80, PART), (half - 80, PART)),
        ((rest, WINDOW), (rest, WINDOW)),
        ((48, PART), (rest - 48, PART)),
        ((2, Y_FIRST, PART), (2, Y_FIRST, PART)),
        ((Y_FIRST // 2, PART), (Y_FIRST // 2, PART)),
    ]
    rings = [[[pltpu.VMEM((3, *shape), b16) for _ in range(2)] for shape in pair] for pair in ring_shapes]
    outs = pl.pallas_call(
        functools.partial(kernel, nz),
        out_shape=(
            jax.ShapeDtypeStruct((rows, depth), b16),
            jax.ShapeDtypeStruct((rows, depth), b16),
            jax.ShapeDtypeStruct((mine, width // 4), f32),
            jax.ShapeDtypeStruct((mine, width // 4), f32),
        ),
        in_specs=[hbm] * 5,
        out_specs=(hbm, hbm, vmem, vmem),
        scratch_shapes=[
            pltpu.VMEM((rows, depth), b16),
            pltpu.VMEM((rows, depth), b16),
            pltpu.VMEM((1, rows), jnp.int32),
            pltpu.VMEM((2, rows, depth), b16),
            pltpu.SemaphoreType.DMA((2,)),
            pltpu.VMEM((2, depth, width), b16),
            pltpu.VMEM((2, depth, rows), b16),
            pltpu.VMEM((2, rows, width), f32),
            pltpu.VMEM((2, rows, 1), f32),
            pltpu.VMEM((2, rows, width), f32),
            pltpu.VMEM((2, 4, rows, width), b16),
            pltpu.VMEM((4, 1, rows), jnp.int32),
            pltpu.VMEM((2, rows, width), b16),
            pltpu.VMEM((2, rows, width), b16),
            pltpu.VMEM((2, 4, chunk, WINDOW), b16),
            pltpu.VMEM((2, 4, chunk, WINDOW), b16),
            pltpu.VMEM((2, 4, chunk, WINDOW), f32),
            pltpu.VMEM((2, half, WINDOW), f32),
            pltpu.VMEM((2, rest, WINDOW), f32),
            pltpu.VMEM((4, Y_FIRST, PART), f32),
            pltpu.VMEM((2, half, PART), f32),
            pltpu.VMEM((2, nz, TILE, PART), b16),
            pltpu.VMEM((2, nz - 1, TILE, PART), b16),
            rings,
            pltpu.SemaphoreType.DMA((3,)),
            pltpu.SemaphoreType.DMA((2,)),
            pltpu.SemaphoreType.DMA((3,)),
            pltpu.SemaphoreType.DMA((3,)),
            pltpu.SemaphoreType.DMA((2, copies)),
            pltpu.SemaphoreType.DMA((2, copies)),
            pltpu.SemaphoreType.DMA((RINGS, 6)),
            pltpu.SemaphoreType.DMA((RINGS, 6)),
        ],
        compiler_params=pltpu.CompilerParams(
            collective_id=0, has_side_effects=True, vmem_limit_bytes=56 * 1024 * 1024),
        cost_estimate=pl.CostEstimate(flops=4_500_000_000, bytes_accessed=8_000_000, transcendentals=300_000),
    )(image_features, text_features, image_weight, text_weight, partner)
    return pl.pallas_call(
        hand_over,
        out_shape=[jax.ShapeDtypeStruct(out.shape, out.dtype) for out in outs],
        in_specs=[vmem] * 4,
        out_specs=[vmem] * 4,
    )(*outs)


def solution(mesh):
    in_specs = (
        P(("wide", "narrow"), None),
        P(("wide", "narrow"), None),
        P(),
        P(),
        P("wide", "narrow"),
    )
    out_specs = (
        P(("wide", "narrow"), None),
        P(("wide", "narrow"), None),
        P("wide", "narrow"),
        P("wide", "narrow"),
    )
    nz = mesh.shape["wide"] // (NX * NYH)
    return jax.shard_map(
        functools.partial(local, nz), mesh=mesh, in_specs=in_specs, out_specs=out_specs, check_vma=False)
```

```python
import functools

import jax
import jax.numpy as jnp
from jax import lax
from jax.experimental import pallas as pl
from jax.experimental.pallas import tpu as pltpu
from jax.sharding import PartitionSpec as P

logit_scale = 10.0
logit_bias = -2.0
norm_eps = 1e-06

NX, NYH = 4, 2
PIECES = 2
WINDOW = 640
CORE_STEP = 512
PART = 384
PART_STEP = 256
TILE = 16
Y_FIRST = 64

OWN_CORE, OWN_CHIP, FORWARD = 0, PIECES, 2 * PIECES
CORE_SUM = 3 * PIECES
Z_SUM = CORE_SUM + 2
RINGS = 6


def kernel(nz, f_i_hbm, f_t_hbm, w_i_hbm, w_t_hbm, partner_hbm, fg_i_hbm, fg_t_hbm, wg_i, wg_t,
           f_i, f_t, partner, fg, fg_sem, w, ft, proj, inv, grad, emb, pairs, pg, pgp,
           f_peer, ft_peer, pg_peer, acc, sums_i, sums_t, sums_y, last, z_out, z_in, ring_bufs,
           f_sem, w_sem, p_send, p_recv, send, recv, ring_send, ring_recv):
    rows, depth = f_i.shape
    width = w.shape[2]
    chunk = depth // NX
    half = chunk // NYH
    mine = half // nz
    quarter = width // 4
    features = (f_i, f_t)
    wide, narrow = lax.axis_index("wide"), lax.axis_index("narrow")
    z, yh, x = lax.rem(wide, nz), lax.rem(wide // nz, NYH), wide // (nz * NYH)
    yl, c = narrow // 2, lax.rem(narrow, 2)

    def device(x=x, yh=yh, z=z, yl=yl, c=c):
        return ((x * NYH + yh) * nz + z, yl * 2 + c)

    core_peer = device(c=1 - c)
    chip_peer = device(yl=1 - yl)
    far_peer = device(yl=1 - yl, c=1 - c)
    block_core, block_chip, block_far = yl * 2 + 1 - c, (1 - yl) * 2 + c, (1 - yl) * 2 + 1 - c
    x_next, x_prev, x_far = lax.rem(x + 1, NX), lax.rem(x + NX - 1, NX), lax.rem(x + 2, NX)
    y = yh * 2 + yl
    y_far, y_next, y_prev = lax.rem(y + 2, 4), lax.rem(y + 1, 4), lax.rem(y + 3, 4)
    x_targets = (x_far, x_next, x_prev, x)
    y_targets = (y_far, y_next, y_prev, y)
    x_pair = (device(x=x_next), device(x=x_prev))
    y_pair = tuple(device(yh=t // 2, yl=lax.rem(t, 2)) for t in (y_next, y_prev))
    z_peers = [(lax.rem(z + d, nz), device(z=lax.rem(z + d, nz))) for d in range(1, nz)]

    barrier = pltpu.get_barrier_semaphore()
    peers = [core_peer, chip_peer, far_peer, *x_pair, device(yh=1 - yh, yl=1 - yl)]
    peers += [peer for _, peer in z_peers]
    for peer in peers:
        pl.semaphore_signal(barrier, inc=1, device_id=peer, device_id_type=pl.DeviceIdType.MESH)

    loads = []
    sources = ((f_t_hbm, f_t), (f_i_hbm, f_i), (partner_hbm, partner))
    feature_loads = [pltpu.make_async_copy(src, dst, f_sem.at[k]) for k, (src, dst) in enumerate(sources)]
    feature_loads[0].start()
    for m, src in ((1, w_t_hbm), (0, w_i_hbm)):
        load = pltpu.make_async_copy(src, w.at[m], w_sem.at[m])
        load.start()
        loads.append(load)
    feature_loads[1].start()
    feature_loads[2].start()

    def remote(src, dst, m, s, peer):
        return pltpu.make_async_remote_copy(
            src_ref=src, dst_ref=dst, send_sem=send.at[m, s], recv_sem=recv.at[m, s],
            device_id=peer, device_id_type=pl.DeviceIdType.MESH)

    started = []

    def go(copy):
        copy.start()
        started.append(copy)
        return copy

    piece = rows // PIECES
    own = {}

    def embed(m):
        p = jnp.dot(features[m][...], w[m], preferred_element_type=jnp.float32)
        i = lax.rsqrt(jnp.sum(p * p, axis=1, keepdims=True) + norm_eps)
        proj[m] = p
        inv[m] = i
        emb[m, narrow] = (p * i).astype(jnp.bfloat16)

    def send_own(m):
        for k in range(PIECES):
            ref = emb.at[m, narrow, pl.ds(k * piece, piece)]
            own[m, 0, k] = go(remote(ref, ref, m, OWN_CORE + k, core_peer))
            own[m, 1, k] = go(remote(ref, ref, m, OWN_CHIP + k, chip_peer))

    def forward(m):
        for k in range(PIECES):
            own[m, 1, k].wait_recv()
            ref = emb.at[m, block_chip, pl.ds(k * piece, piece)]
            own[m, 2, k] = go(remote(ref, ref, m, FORWARD + k, core_peer))

    def arrived(m, kind):
        for k in range(PIECES):
            own[m, kind, k].wait_recv()

    feature_loads[0].wait()
    loads[0].wait()
    embed(1)
    pl.semaphore_wait(barrier, len(peers))
    send_own(1)
    feature_loads[2].wait()
    pairs[narrow] = partner[...]
    pair_copies = []
    for s, peer in enumerate((core_peer, chip_peer, far_peer)):
        copy = pltpu.make_async_remote_copy(
            src_ref=pairs.at[narrow], dst_ref=pairs.at[narrow], send_sem=p_send.at[s], recv_sem=p_recv.at[s],
            device_id=peer, device_id_type=pl.DeviceIdType.MESH)
        pair_copies.append(go(copy))
    feature_loads[1].wait()
    loads[1].wait()
    embed(0)
    send_own(0)
    feature_copies = {m: go(remote(features[m], f_peer.at[m], m, CORE_SUM, core_peer)) for m in (1, 0)}

    for m in (0, 1):
        ft[m] = features[m][...].T
    for m in (1, 0):
        feature_copies[m].wait_recv()
        ft_peer[m] = f_peer[m].T

    down = lax.broadcasted_iota(jnp.int32, (rows, rows), 0)
    along = lax.broadcasted_iota(jnp.int32, (rows, rows), 1)
    partner_down = jnp.sum(
        jnp.where(down == along, partner[...].astype(jnp.float32), 0.0), axis=1, keepdims=True
    ).astype(jnp.int32)

    def add_block(m, block, first):
        other = emb[1 - m, block]
        logits = logit_scale * lax.dot_general(
            emb[m, narrow], other, (((1,), (1,)), ((), ())), preferred_element_type=jnp.float32
        ) + logit_bias
        if m == 0:
            match = partner_down == block * rows + along
        else:
            match = pairs[block] == narrow * rows + down
        pair = jnp.where(match, -logit_scale, logit_scale) * jax.nn.sigmoid(jnp.where(match, -logits, logits))
        part = jnp.dot(pair.astype(jnp.bfloat16), other, preferred_element_type=jnp.float32)
        grad[m] = part if first else grad[m] + part

    def project_back(m):
        p, i, g = proj[m], inv[m], grad[m]
        total = jnp.sum(p * g, axis=1, keepdims=True)
        value = i * g - p * (i * i * i * total)
        value = value.astype(jnp.bfloat16)
        pg[m] = value
        q = quarter
        pgp[m] = jnp.concatenate([value[:, :q], value[:, 2 * q:3 * q], value[:, q:2 * q], value[:, 3 * q:]], axis=1)

    fg_copies = []

    def feature_grad(m, out):
        fg[m] = lax.dot_general(
            pg[m], w[m], (((1,), (1,)), ((), ())), preferred_element_type=jnp.float32
        ).astype(jnp.bfloat16)
        copy = pltpu.make_async_copy(fg.at[m], out, fg_sem.at[m])
        copy.start()
        fg_copies.append(copy)

    core_copies, z_copies = {}, {}

    def window(core):
        return pl.ds(pl.multiple_of(core * CORE_STEP, 128), WINDOW)

    def core_start(m):
        core_copies[m] = go(remote(pgp.at[m, :, window(1 - c)], pg_peer.at[m], m, CORE_SUM + 1, core_peer))

    def chip_share(m, k):
        block = pl.ds(pl.multiple_of(x_targets[k] * chunk, 16), chunk)
        part = jnp.dot(ft[m, block, :], pgp[m, :, window(c)], preferred_element_type=jnp.float32)
        if k == 0:
            core_copies[m].wait_recv()
        acc[m, k] = part + jnp.dot(ft_peer[m, block, :], pg_peer[m], preferred_element_type=jnp.float32)

    class Ring:
        def __init__(self, n, pair, value):
            self.n, self.pair, self.value, self.copies = n, pair, value, {}

        def push(self, h, kind, peer, value):
            out, into = ring_bufs[self.n][h]
            out[kind] = value.astype(jnp.bfloat16)
            s = h * 3 + kind
            self.copies[h, kind] = go(pltpu.make_async_remote_copy(
                src_ref=out.at[kind], dst_ref=into.at[kind],
                send_sem=ring_send.at[self.n, s], recv_sem=ring_recv.at[self.n, s],
                device_id=peer, device_id_type=pl.DeviceIdType.MESH))

        def pull(self, h, kind):
            self.copies[h, kind].wait_recv()
            return ring_bufs[self.n][h][1][kind].astype(jnp.float32)

        def relay(self, h):
            self.push(h, 0, self.pair[h], self.value(0, h))

        def direct(self, h):
            self.push(h, 1, self.pair[1 - h], self.value(2 - h, h))

        def both(self):
            for h in range(2):
                self.push(h, 2, self.pair[h], self.value(1 + h, h) + self.pull(h, 0))

        def total(self, h):
            return self.value(3, h) + self.pull(h, 1) + self.pull(h, 2)

    def x_first(m, low):
        return lambda k, h: acc[m, k, h * half + low:(h + 1) * half, :]

    def column_part(l):
        return pl.ds(pl.multiple_of(l * PART_STEP, 128), PART)

    def y_second(sums, cuts):
        def value(k, h):
            t = y_targets[k]
            return sums[t // 2, cuts[h]:cuts[h + 1], column_part(lax.rem(t, 2))]
        return value

    def y_first(k, h):
        t = y_targets[k]
        block = pl.ds(pl.multiple_of((t // 2) * half, 8), Y_FIRST)
        return acc[1, 2 * h:2 * h + 2, block, column_part(lax.rem(t, 2))]

    def x_second(k, h):
        n = Y_FIRST // 2
        return sums_y[k, h * n:(h + 1) * n, :]

    cuts_i, cuts_t = (0, 80, half), (0, 48, half - Y_FIRST)
    ring_ix = Ring(0, x_pair, x_first(0, 0))
    ring_iy = Ring(1, y_pair, y_second(sums_i, cuts_i))
    ring_tx = Ring(2, x_pair, x_first(1, Y_FIRST))
    ring_txy = Ring(3, y_pair, y_second(sums_t, cuts_t))
    ring_ty = Ring(4, y_pair, y_first)
    ring_tyx = Ring(5, x_pair, x_second)

    def begin(ring):
        ring.relay(0)
        ring.relay(1)
        ring.direct(1)
        ring.direct(0)

    spare = PART - quarter
    segments = quarter // spare
    rest = mine - TILE

    def z_start(m):
        total = last[m]
        offset = (quarter - PART_STEP) * (yl + 2 * c)
        total = pltpu.roll(total, lax.rem(PART - offset, PART), 1)
        row = lax.broadcasted_iota(jnp.int32, (nz * TILE, half), 0)
        column = lax.broadcasted_iota(jnp.int32, (nz * TILE, half), 1)
        which, within = row // TILE, lax.rem(row, TILE)

        def pick(chosen, source, value):
            spread = jnp.where(chosen & (column == which * mine + source), 1.0, 0.0).astype(jnp.bfloat16)
            return jnp.dot(spread, value.astype(jnp.bfloat16), preferred_element_type=jnp.float32)

        body = pick(within < TILE, within, total)
        tail = jnp.zeros_like(body)
        for s in range(segments):
            moved = pltpu.roll(total, quarter - s * spare, 1)
            chosen = (within < rest * segments) & (lax.rem(within, segments) == s)
            tail = tail + pick(chosen, TILE + within // segments, moved)
        lane = lax.broadcasted_iota(jnp.int32, body.shape, 1)
        packed = jnp.where(lane < quarter, body, tail).astype(jnp.bfloat16)
        for d in range(nz):
            z_out[m, d] = packed[d * TILE:(d + 1) * TILE]
        for s, (zd, peer) in enumerate(z_peers):
            z_copies[m, s] = go(remote(z_out.at[m, zd], z_in.at[m, s], m, Z_SUM + s, peer))

    def z_finish(m, out):
        total = z_out[m, z].astype(jnp.float32)
        for s in range(nz - 1):
            z_copies[m, s].wait_recv()
            total = total + z_in[m, s].astype(jnp.float32)
        out[:TILE, :] = total[:, :quarter]
        for r in range(rest):
            rows_of = [total[r * segments + s:r * segments + s + 1, quarter:] for s in range(segments)]
            out[TILE + r:TILE + r + 1, :] = jnp.concatenate(rows_of, axis=1)

    add = add_block
    add(0, narrow, True)
    pair_copies[0].wait_recv()
    add(1, narrow, True)
    arrived(1, 0)
    add(0, block_core, False)
    arrived(0, 0)
    add(1, block_core, False)

    forward(1)
    add(0, block_chip, False)
    arrived(1, 2)
    add(0, block_far, False)
    project_back(0)
    core_start(0)
    chip_share(0, 0)
    ring_ix.relay(0)
    ring_ix.relay(1)
    chip_share(0, 1)
    ring_ix.direct(1)
    chip_share(0, 2)
    ring_ix.direct(0)
    chip_share(0, 3)
    feature_grad(0, fg_i_hbm)

    forward(0)
    pair_copies[1].wait_recv()
    pair_copies[2].wait_recv()
    add(1, block_chip, False)
    arrived(0, 2)
    add(1, block_far, False)
    project_back(1)
    core_start(1)
    ring_ix.both()
    chip_share(1, 0)
    ring_tx.relay(0)
    ring_tx.relay(1)
    chip_share(1, 1)
    ring_ty.relay(0)
    ring_ty.direct(0)
    ring_tx.direct(1)
    chip_share(1, 2)
    ring_tx.direct(0)
    chip_share(1, 3)
    ring_ty.relay(1)
    ring_ty.direct(1)

    for h in range(2):
        sums_i[h] = ring_ix.total(h)
    begin(ring_iy)
    ring_tx.both()
    ring_ty.both()
    ring_iy.both()
    feature_grad(1, fg_t_hbm)
    for h in range(2):
        sums_t[h] = ring_tx.total(h)
    begin(ring_txy)
    for h in range(2):
        sums_y[2 * h:2 * h + 2] = ring_ty.total(h)
    begin(ring_tyx)
    for h in range(2):
        last[0, cuts_i[h]:cuts_i[h + 1]] = ring_iy.total(h)
    z_start(0)
    ring_txy.both()
    ring_tyx.both()
    for h in range(2):
        n = Y_FIRST // 2
        last[1, h * n:(h + 1) * n] = ring_tyx.total(h)
    for h in range(2):
        last[1, Y_FIRST + cuts_t[h]:Y_FIRST + cuts_t[h + 1]] = ring_txy.total(h)
    z_start(1)
    z_finish(0, wg_i)
    z_finish(1, wg_t)
    for copy in fg_copies:
        copy.wait()
    for copy in started:
        copy.wait_send()


def hand_over(a, b, c, d, a_out, b_out, c_out, d_out):
    a_out[...], b_out[...], c_out[...], d_out[...] = a[...], b[...], c[...], d[...]


def local(nz, image_features, text_features, image_weight, text_weight, partner):
    rows, depth = image_features.shape
    width = image_weight.shape[1]
    chunk = depth // NX
    half = chunk // NYH
    mine = half // nz
    b16, f32 = jnp.bfloat16, jnp.float32
    vmem = pl.BlockSpec(memory_space=pltpu.VMEM)
    hbm = pl.BlockSpec(memory_space=pl.ANY)
    copies = Z_SUM + nz - 1
    rest = half - Y_FIRST
    ring_shapes = [
        ((half, WINDOW), (half, WINDOW)),
        ((80, PART), (half - 80, PART)),
        ((rest, WINDOW), (rest, WINDOW)),
        ((48, PART), (rest - 48, PART)),
        ((2, Y_FIRST, PART), (2, Y_FIRST, PART)),
        ((Y_FIRST // 2, PART), (Y_FIRST // 2, PART)),
    ]
    rings = [[[pltpu.VMEM((3, *shape), b16) for _ in range(2)] for shape in pair] for pair in ring_shapes]
    outs = pl.pallas_call(
        functools.partial(kernel, nz),
        out_shape=(
            jax.ShapeDtypeStruct((rows, depth), b16),
            jax.ShapeDtypeStruct((rows, depth), b16),
            jax.ShapeDtypeStruct((mine, width // 4), f32),
            jax.ShapeDtypeStruct((mine, width // 4), f32),
        ),
        in_specs=[hbm] * 5,
        out_specs=(hbm, hbm, vmem, vmem),
        scratch_shapes=[
            pltpu.VMEM((rows, depth), b16),
            pltpu.VMEM((rows, depth), b16),
            pltpu.VMEM((1, rows), jnp.int32),
            pltpu.VMEM((2, rows, depth), b16),
            pltpu.SemaphoreType.DMA((2,)),
            pltpu.VMEM((2, depth, width), b16),
            pltpu.VMEM((2, depth, rows), b16),
            pltpu.VMEM((2, rows, width), f32),
            pltpu.VMEM((2, rows, 1), f32),
            pltpu.VMEM((2, rows, width), f32),
            pltpu.VMEM((2, 4, rows, width), b16),
            pltpu.VMEM((4, 1, rows), jnp.int32),
            pltpu.VMEM((2, rows, width), b16),
            pltpu.VMEM((2, rows, width), b16),
            pltpu.VMEM((2, rows, depth), b16),
            pltpu.VMEM((2, depth, rows), b16),
            pltpu.VMEM((2, rows, WINDOW), b16),
            pltpu.VMEM((2, 4, chunk, WINDOW), f32),
            pltpu.VMEM((2, half, WINDOW), f32),
            pltpu.VMEM((2, rest, WINDOW), f32),
            pltpu.VMEM((4, Y_FIRST, PART), f32),
            pltpu.VMEM((2, half, PART), f32),
            pltpu.VMEM((2, nz, TILE, PART), b16),
            pltpu.VMEM((2, nz - 1, TILE, PART), b16),
            rings,
            pltpu.SemaphoreType.DMA((3,)),
            pltpu.SemaphoreType.DMA((2,)),
            pltpu.SemaphoreType.DMA((3,)),
            pltpu.SemaphoreType.DMA((3,)),
            pltpu.SemaphoreType.DMA((2, copies)),
            pltpu.SemaphoreType.DMA((2, copies)),
            pltpu.SemaphoreType.DMA((RINGS, 6)),
            pltpu.SemaphoreType.DMA((RINGS, 6)),
        ],
        compiler_params=pltpu.CompilerParams(
            collective_id=0, has_side_effects=True, vmem_limit_bytes=56 * 1024 * 1024),
        cost_estimate=pl.CostEstimate(flops=4_500_000_000, bytes_accessed=8_000_000, transcendentals=300_000),
    )(image_features, text_features, image_weight, text_weight, partner)
    return pl.pallas_call(
        hand_over,
        out_shape=[jax.ShapeDtypeStruct(out.shape, out.dtype) for out in outs],
        in_specs=[vmem] * 4,
        out_specs=[vmem] * 4,
    )(*outs)


def solution(mesh):
    in_specs = (
        P(("wide", "narrow"), None),
        P(("wide", "narrow"), None),
        P(),
        P(),
        P("wide", "narrow"),
    )
    out_specs = (
        P(("wide", "narrow"), None),
        P(("wide", "narrow"), None),
        P("wide", "narrow"),
        P("wide", "narrow"),
    )
    nz = mesh.shape["wide"] // (NX * NYH)
    return jax.shard_map(
        functools.partial(local, nz), mesh=mesh, in_specs=in_specs, out_specs=out_specs, check_vma=False)
```

```python
import functools

import jax
import jax.numpy as jnp
from jax import lax
from jax.experimental import pallas as pl
from jax.experimental.pallas import tpu as pltpu
from jax.sharding import PartitionSpec as P

logit_scale = 10.0
logit_bias = -2.0
norm_eps = 1e-06

NX, NYH = 4, 2
PIECES = 2
WINDOW = 640
CORE_STEP = 512
PART = 384
PART_STEP = 256
TILE = 16
CUT = 80
Y_FIRST = 64

OWN_CORE, OWN_CHIP, FORWARD = 0, PIECES, 2 * PIECES
CORE_SUM = 3 * PIECES
Z_SUM = CORE_SUM + 2
RINGS = 4


Z_ORDER = (4, 3, -3, 2, -2, 1, -1, 0)


def kernel(nz, f_i_hbm, f_t_hbm, w_i_hbm, w_t_hbm, partner_hbm, fg_i_hbm, fg_t_hbm, wg_i, wg_t,
           f_i, f_t, partner, fg, fg_sem, f_sem, w, ft, ft_z, proj, inv, grad, emb, pairs, pg, pgp,
           f_peer, ft_peer, ft_z_peer, pg_peer, acc_i, acc, plane_out, plane_in, sums_t, sums_y, last, z_out, z_in,
           long_bufs, ring_bufs, w_sem, p_send, p_recv, plane_send, plane_recv, send, recv, long_send, long_recv, ring_send, ring_recv):
    rows, depth = f_i.shape
    width = w.shape[2]
    chunk = depth // NX
    half = chunk // NYH
    mine = half // nz
    quarter = width // 4
    features = (f_i, f_t)
    wide, narrow = lax.axis_index("wide"), lax.axis_index("narrow")
    z, yh, x = lax.rem(wide, nz), lax.rem(wide // nz, NYH), wide // (nz * NYH)
    yl, c = narrow // 2, lax.rem(narrow, 2)

    def device(x=x, yh=yh, z=z, yl=yl, c=c):
        return ((x * NYH + yh) * nz + z, yl * 2 + c)

    core_peer = device(c=1 - c)
    chip_peer = device(yl=1 - yl)
    far_peer = device(yl=1 - yl, c=1 - c)
    block_core, block_chip, block_far = yl * 2 + 1 - c, (1 - yl) * 2 + c, (1 - yl) * 2 + 1 - c
    x_next, x_prev, x_far = lax.rem(x + 1, NX), lax.rem(x + NX - 1, NX), lax.rem(x + 2, NX)
    y = yh * 2 + yl
    y_far, y_next, y_prev = lax.rem(y + 2, 4), lax.rem(y + 1, 4), lax.rem(y + 3, 4)
    x_targets = (x_far, x_next, x_prev, x)
    y_targets = (y_far, y_next, y_prev, y)
    x_pair = (device(x=x_next), device(x=x_prev))
    y_pair = tuple(device(yh=t // 2, yl=lax.rem(t, 2)) for t in (y_next, y_prev))
    z_peers = [(lax.rem(z + d, nz), device(z=lax.rem(z + d, nz))) for d in range(1, nz)]

    barrier = pltpu.get_barrier_semaphore()
    plane_peers = []
    for dx in (2, 1, 3, 0):
        for dy in (2, 1, 3, 0):
            if dx or dy:
                xd, yd = lax.rem(x + dx, NX), lax.rem(y + dy, 4)
                plane_peers.append((xd * NYH + yd // 2, lax.rem(yd, 2), device(x=xd, yh=yd // 2, yl=lax.rem(yd, 2))))
    peers = [core_peer, far_peer, *(peer for _, _, peer in plane_peers)]
    peers += [peer for _, peer in z_peers]
    for peer in peers:
        pl.semaphore_signal(barrier, inc=1, device_id=peer, device_id_type=pl.DeviceIdType.MESH)

    loads = []
    sources = ((f_t_hbm, f_t), (f_i_hbm, f_i), (partner_hbm, partner))
    feature_loads = [pltpu.make_async_copy(src, dst, f_sem.at[k]) for k, (src, dst) in enumerate(sources)]
    feature_loads[0].start()
    for m, src in ((1, w_t_hbm), (0, w_i_hbm)):
        load = pltpu.make_async_copy(src, w.at[m], w_sem.at[m])
        load.start()
        loads.append(load)
    feature_loads[1].start()
    feature_loads[2].start()

    def remote(src, dst, m, s, peer):
        return pltpu.make_async_remote_copy(
            src_ref=src, dst_ref=dst, send_sem=send.at[m, s], recv_sem=recv.at[m, s],
            device_id=peer, device_id_type=pl.DeviceIdType.MESH)

    started = []

    def go(copy):
        copy.start()
        started.append(copy)
        return copy

    piece = rows // PIECES
    own = {}

    def embed(m):
        p = jnp.dot(features[m][...], w[m], preferred_element_type=jnp.float32)
        i = lax.rsqrt(jnp.sum(p * p, axis=1, keepdims=True) + norm_eps)
        proj[m] = p
        inv[m] = i
        emb[m, narrow] = (p * i).astype(jnp.bfloat16)

    def send_own(m):
        for k in range(PIECES):
            ref = emb.at[m, narrow, pl.ds(k * piece, piece)]
            own[m, 0, k] = go(remote(ref, ref, m, OWN_CORE + k, core_peer))
            own[m, 1, k] = go(remote(ref, ref, m, OWN_CHIP + k, chip_peer))

    def forward(m, k):
        own[m, 1, k].wait_recv()
        ref = emb.at[m, block_chip, pl.ds(k * piece, piece)]
        own[m, 2, k] = go(remote(ref, ref, m, FORWARD + k, core_peer))

    def arrived(m, kind):
        for k in range(PIECES):
            own[m, kind, k].wait_recv()

    feature_loads[0].wait()
    loads[0].wait()
    embed(1)
    pl.semaphore_wait(barrier, len(peers))
    send_own(1)
    feature_loads[2].wait()
    pairs[narrow] = partner[...]
    pair_copies = []
    for s, peer in enumerate((core_peer, chip_peer, far_peer)):
        copy = pltpu.make_async_remote_copy(
            src_ref=pairs.at[narrow], dst_ref=pairs.at[narrow], send_sem=p_send.at[s], recv_sem=p_recv.at[s],
            device_id=peer, device_id_type=pl.DeviceIdType.MESH)
        pair_copies.append(go(copy))
    feature_loads[1].wait()
    loads[1].wait()
    embed(0)
    send_own(0)
    feature_copies = {m: go(remote(features[m], f_peer.at[m], m, CORE_SUM, core_peer)) for m in (1, 0)}

    ft[...] = f_t[...].T
    feature_copies[1].wait_recv()
    ft_peer[...] = f_peer[1].T
    feature_copies[0].wait_recv()
    row = lax.broadcasted_iota(jnp.int32, (half, 1), 0)
    source = (row // mine) * half + lax.rem(row, mine)
    column = lax.broadcasted_iota(jnp.int32, (half, depth), 1)
    for d in range(nz):
        order = jnp.where(column == source + d * mine, 1.0, 0.0).astype(jnp.bfloat16)
        for left, right in ((ft_z, f_i[...]), (ft_z_peer, f_peer[0])):
            left[d] = lax.dot_general(
                order, right, (((1,), (1,)), ((), ())), preferred_element_type=jnp.float32
            ).astype(jnp.bfloat16)

    down = lax.broadcasted_iota(jnp.int32, (rows, rows), 0)
    along = lax.broadcasted_iota(jnp.int32, (rows, rows), 1)
    partner_down = jnp.sum(
        jnp.where(down == along, partner[...].astype(jnp.float32), 0.0), axis=1, keepdims=True
    ).astype(jnp.int32)

    def add_block(m, block, first):
        other = emb[1 - m, block]
        logits = logit_scale * lax.dot_general(
            emb[m, narrow], other, (((1,), (1,)), ((), ())), preferred_element_type=jnp.float32
        ) + logit_bias
        if m == 0:
            match = partner_down == block * rows + along
        else:
            match = pairs[block] == narrow * rows + down
        pair = jnp.where(match, -logit_scale, logit_scale) * jax.nn.sigmoid(jnp.where(match, -logits, logits))
        part = jnp.dot(pair.astype(jnp.bfloat16), other, preferred_element_type=jnp.float32)
        grad[m] = part if first else grad[m] + part

    def project_back(m):
        p, i, g = proj[m], inv[m], grad[m]
        total = jnp.sum(p * g, axis=1, keepdims=True)
        value = i * g - p * (i * i * i * total)
        value = value.astype(jnp.bfloat16)
        pg[m] = value
        q = quarter
        pgp[m] = jnp.concatenate([value[:, :q], value[:, 2 * q:3 * q], value[:, q:2 * q], value[:, 3 * q:]], axis=1)

    fg_copies = []

    def feature_grad(m, out):
        fg[m] = lax.dot_general(
            pg[m], w[m], (((1,), (1,)), ((), ())), preferred_element_type=jnp.float32
        ).astype(jnp.bfloat16)
        copy = pltpu.make_async_copy(fg.at[m], out, fg_sem.at[m])
        copy.start()
        fg_copies.append(copy)

    core_copies, z_copies = {}, {}

    def window(core):
        return pl.ds(pl.multiple_of(core * CORE_STEP, 128), WINDOW)

    def core_start(m):
        core_copies[m] = go(remote(pgp.at[m, :, window(1 - c)], pg_peer.at[m], m, CORE_SUM + 1, core_peer))

    def chip_share(m, k):
        if m == 0:
            place = lax.rem(z + Z_ORDER[k] + nz, nz)
            own_left, peer_left, total = ft_z[place], ft_z_peer[place], acc_i
        else:
            block = pl.ds(pl.multiple_of(x_targets[k] * chunk, 16), chunk)
            own_left, peer_left, total = ft[block, :], ft_peer[block, :], acc
        part = jnp.dot(own_left, pgp[m, :, window(c)], preferred_element_type=jnp.float32)
        if k == 0:
            core_copies[m].wait_recv()
        total[k] = part + jnp.dot(peer_left, pg_peer[m], preferred_element_type=jnp.float32)

    z_pair = (device(z=lax.rem(z + 1, nz)), device(z=lax.rem(z + nz - 1, nz)))
    spans = (pl.ds(0, CUT), pl.ds(CUT, half - CUT))
    long_copies = {}

    def own_part(d, h):
        return acc_i[Z_ORDER.index(d), spans[h], :]

    def long_push(way, hops, far):
        h = way if far else 1 - way
        out, into = long_bufs[way][h]
        value = own_part(hops if way == 0 or hops == nz // 2 else -hops, h)
        first = nz // 2 if far else nz // 2 - 1
        if hops < first:
            value = value + long_pull(way, hops + 1, far)
        slot = first - hops
        out[slot] = value.astype(jnp.bfloat16)
        s = 2 * slot + (0 if far else 1)
        long_copies[way, hops, far] = go(pltpu.make_async_remote_copy(
            src_ref=out.at[slot], dst_ref=into.at[slot], send_sem=long_send.at[way, s], recv_sem=long_recv.at[way, s],
            device_id=z_pair[way], device_id_type=pl.DeviceIdType.MESH))

    def long_pull(way, hops, far):
        long_copies[way, hops, far].wait_recv()
        h = way if far else 1 - way
        first = nz // 2 if far else nz // 2 - 1
        return long_bufs[way][h][1][first - hops].astype(jnp.float32)

    def long_step(hops, far):
        for way in range(2):
            long_push(way, hops, far)

    class Ring:
        def __init__(self, n, pair, value):
            self.n, self.pair, self.value, self.copies = n, pair, value, {}

        def push(self, h, kind, peer, value):
            out, into = ring_bufs[self.n][h]
            out[kind] = value.astype(jnp.bfloat16)
            s = h * 3 + kind
            self.copies[h, kind] = go(pltpu.make_async_remote_copy(
                src_ref=out.at[kind], dst_ref=into.at[kind],
                send_sem=ring_send.at[self.n, s], recv_sem=ring_recv.at[self.n, s],
                device_id=peer, device_id_type=pl.DeviceIdType.MESH))

        def pull(self, h, kind):
            self.copies[h, kind].wait_recv()
            return ring_bufs[self.n][h][1][kind].astype(jnp.float32)

        def relay(self, h):
            self.push(h, 0, self.pair[h], self.value(0, h))

        def direct(self, h):
            self.push(h, 1, self.pair[1 - h], self.value(2 - h, h))

        def both(self):
            for h in range(2):
                self.push(h, 2, self.pair[h], self.value(1 + h, h) + self.pull(h, 0))

        def total(self, h):
            return self.value(3, h) + self.pull(h, 1) + self.pull(h, 2)

    def x_first(k, h):
        return acc[k, h * half + Y_FIRST:(h + 1) * half, :]

    def column_part(l):
        return pl.ds(pl.multiple_of(l * PART_STEP, 128), PART)

    def y_second(sums, cuts):
        def value(k, h):
            t = y_targets[k]
            return sums[t // 2, cuts[h]:cuts[h + 1], column_part(lax.rem(t, 2))]
        return value

    def y_first(k, h):
        t = y_targets[k]
        block = pl.ds(pl.multiple_of((t // 2) * half, 8), Y_FIRST)
        return acc[2 * h:2 * h + 2, block, column_part(lax.rem(t, 2))]

    def x_second(k, h):
        n = Y_FIRST // 2
        return sums_y[k, h * n:(h + 1) * n, :]

    cuts_t = (0, 48, half - Y_FIRST)
    ring_tx = Ring(0, x_pair, x_first)
    ring_txy = Ring(1, y_pair, y_second(sums_t, cuts_t))
    ring_ty = Ring(2, y_pair, y_first)
    ring_tyx = Ring(3, x_pair, x_second)

    def begin(ring):
        ring.relay(0)
        ring.relay(1)
        ring.direct(1)
        ring.direct(0)

    spare = PART - quarter
    segments = quarter // spare
    rest = mine - TILE

    def offset_of(l):
        return (quarter - PART_STEP) * (l + 2 * c)

    def pack(total, l):
        total = total.astype(jnp.bfloat16)
        row = lax.broadcasted_iota(jnp.int32, (8 * TILE, half), 0)
        column = lax.broadcasted_iota(jnp.int32, (8 * TILE, half), 1)
        which, within = row // TILE, lax.rem(row, TILE)

        def pick(chosen, source):
            spread = jnp.where(chosen & (column == which * mine + source), 1.0, 0.0).astype(jnp.bfloat16)
            return jnp.dot(spread, total, preferred_element_type=jnp.float32)

        body = pick(within < TILE, within)
        tail = pick(within < rest * segments, TILE + within // segments)
        row = lax.broadcasted_iota(jnp.int32, (8 * TILE, 1), 0)
        segment = lax.rem(lax.rem(row, TILE), segments)
        moved = [pltpu.roll(tail, quarter - s * spare, 1) for s in range(segments)]
        chosen = moved[0]
        for s in range(1, segments):
            chosen = jnp.where(segment == s, moved[s], chosen)
        lane = lax.rem(lax.broadcasted_iota(jnp.int32, body.shape, 1) + PART - offset_of(l), PART)
        return jnp.where(lane < quarter, body, chosen).astype(jnp.bfloat16)

    def unpack(total, out):
        total = pltpu.roll(total, lax.rem(PART - offset_of(yl), PART), 1)
        out[:TILE, :] = total[:, :quarter]
        for r in range(rest):
            pieces = [total[r * segments + s:r * segments + s + 1, quarter:] for s in range(segments)]
            out[TILE + r:TILE + r + 1, :] = jnp.concatenate(pieces, axis=1)

    plane_copies = []

    def plane_pack():
        low = own_part(0, 0) + long_pull(0, 1, True) + long_pull(1, 1, False)
        high = own_part(0, 1) + long_pull(0, 1, False) + long_pull(1, 1, True)
        total = jnp.concatenate([low, high], axis=0)
        for l in range(2):
            packed = pack(total[:, l * PART_STEP:l * PART_STEP + PART], l)
            for d in range(8):
                plane_out[l, d] = packed[d * TILE:(d + 1) * TILE]

    def plane_start():
        for s, (place, l, peer) in enumerate(plane_peers):
            plane_copies.append(go(pltpu.make_async_remote_copy(
                src_ref=plane_out.at[l, place], dst_ref=plane_in.at[s],
                send_sem=plane_send.at[s], recv_sem=plane_recv.at[s],
                device_id=peer, device_id_type=pl.DeviceIdType.MESH)))

    def plane_finish(out):
        total = plane_out[yl, x * NYH + yh].astype(jnp.float32)
        for s, copy in enumerate(plane_copies):
            copy.wait_recv()
            total = total + plane_in[s].astype(jnp.float32)
        unpack(total, out)

    def z_start():
        packed = pack(last[...], yl)
        for d in range(nz):
            z_out[d] = packed[d * TILE:(d + 1) * TILE]
        for s, (zd, peer) in enumerate(z_peers):
            z_copies[s] = go(remote(z_out.at[zd], z_in.at[s], 1, Z_SUM + s, peer))

    def z_finish(out):
        total = z_out[z].astype(jnp.float32)
        for s in range(nz - 1):
            z_copies[s].wait_recv()
            total = total + z_in[s].astype(jnp.float32)
        unpack(total, out)

    add = add_block
    add(0, narrow, True)
    pair_copies[0].wait_recv()
    add(1, narrow, True)
    arrived(1, 0)
    add(0, block_core, False)
    arrived(0, 0)
    add(1, block_core, False)

    forward(1, 0)
    forward(1, 1)
    add(0, block_chip, False)
    arrived(1, 2)
    add(0, block_far, False)
    project_back(0)
    half_z = nz // 2
    core_start(0)
    chip_share(0, 0)
    long_step(half_z, True)
    for way in range(2):
        chip_share(0, 1 + way)
        long_push(way, half_z - 1, False)
    for k in range(3, nz):
        chip_share(0, k)
    forward(0, 0)
    feature_grad(0, fg_i_hbm)
    long_step(3, True)

    forward(0, 1)
    pair_copies[1].wait_recv()
    pair_copies[2].wait_recv()
    long_step(2, False)
    add(1, block_chip, False)
    arrived(0, 2)
    add(1, block_far, False)
    project_back(1)
    core_start(1)
    chip_share(1, 0)
    ring_tx.relay(0)
    ring_tx.relay(1)
    chip_share(1, 1)
    ring_ty.relay(0)
    ring_ty.direct(0)
    ring_tx.direct(1)
    chip_share(1, 2)
    ring_tx.direct(0)
    long_step(2, True)
    chip_share(1, 3)
    ring_ty.relay(1)
    ring_ty.direct(1)
    long_step(1, False)
    long_step(1, True)

    ring_tx.both()
    ring_ty.both()
    feature_grad(1, fg_t_hbm)
    for h in range(2):
        sums_t[h] = ring_tx.total(h)
    begin(ring_txy)
    for h in range(2):
        sums_y[2 * h:2 * h + 2] = ring_ty.total(h)
    begin(ring_tyx)
    plane_pack()
    ring_txy.both()
    ring_tyx.both()
    plane_start()
    for h in range(2):
        n = Y_FIRST // 2
        last[h * n:(h + 1) * n] = ring_tyx.total(h)
    for h in range(2):
        last[Y_FIRST + cuts_t[h]:Y_FIRST + cuts_t[h + 1]] = ring_txy.total(h)
    z_start()
    plane_finish(wg_i)
    z_finish(wg_t)
    for copy in fg_copies:
        copy.wait()
    for copy in started:
        copy.wait_send()


def hand_over(a, b, c, d, a_out, b_out, c_out, d_out):
    a_out[...], b_out[...], c_out[...], d_out[...] = a[...], b[...], c[...], d[...]


def local(nz, image_features, text_features, image_weight, text_weight, partner):
    rows, depth = image_features.shape
    width = image_weight.shape[1]
    chunk = depth // NX
    half = chunk // NYH
    mine = half // nz
    b16, f32 = jnp.bfloat16, jnp.float32
    vmem = pl.BlockSpec(memory_space=pltpu.VMEM)
    hbm = pl.BlockSpec(memory_space=pl.ANY)
    copies = Z_SUM + nz - 1
    rest = half - Y_FIRST
    ring_shapes = [
        ((rest, WINDOW), (rest, WINDOW)),
        ((48, PART), (rest - 48, PART)),
        ((2, Y_FIRST, PART), (2, Y_FIRST, PART)),
        ((Y_FIRST // 2, PART), (Y_FIRST // 2, PART)),
    ]
    rings = [[[pltpu.VMEM((3, *shape), b16) for _ in range(2)] for shape in pair] for pair in ring_shapes]
    long_rows, hops = (CUT, half - CUT), nz // 2
    longs = [
        [[pltpu.VMEM((hops if h == way else hops - 1, long_rows[h], WINDOW), b16) for _ in range(2)] for h in range(2)]
        for way in range(2)
    ]
    outs = pl.pallas_call(
        functools.partial(kernel, nz),
        out_shape=(
            jax.ShapeDtypeStruct((rows, depth), b16),
            jax.ShapeDtypeStruct((rows, depth), b16),
            jax.ShapeDtypeStruct((mine, width // 4), f32),
            jax.ShapeDtypeStruct((mine, width // 4), f32),
        ),
        in_specs=[hbm] * 5,
        out_specs=(hbm, hbm, vmem, vmem),
        scratch_shapes=[
            pltpu.VMEM((rows, depth), b16),
            pltpu.VMEM((rows, depth), b16),
            pltpu.VMEM((1, rows), jnp.int32),
            pltpu.VMEM((2, rows, depth), b16),
            pltpu.SemaphoreType.DMA((2,)),
            pltpu.SemaphoreType.DMA((3,)),
            pltpu.VMEM((2, depth, width), b16),
            pltpu.VMEM((depth, rows), b16),
            pltpu.VMEM((nz, half, rows), b16),
            pltpu.VMEM((2, rows, width), f32),
            pltpu.VMEM((2, rows, 1), f32),
            pltpu.VMEM((2, rows, width), f32),
            pltpu.VMEM((2, 4, rows, width), b16),
            pltpu.VMEM((4, 1, rows), jnp.int32),
            pltpu.VMEM((2, rows, width), b16),
            pltpu.VMEM((2, rows, width), b16),
            pltpu.VMEM((2, rows, depth), b16),
            pltpu.VMEM((depth, rows), b16),
            pltpu.VMEM((nz, half, rows), b16),
            pltpu.VMEM((2, rows, WINDOW), b16),
            pltpu.VMEM((nz, half, WINDOW), f32),
            pltpu.VMEM((4, chunk, WINDOW), f32),
            pltpu.VMEM((2, 8, TILE, PART), b16),
            pltpu.VMEM((15, TILE, PART), b16),
            pltpu.VMEM((2, rest, WINDOW), f32),
            pltpu.VMEM((4, Y_FIRST, PART), f32),
            pltpu.VMEM((half, PART), f32),
            pltpu.VMEM((nz, TILE, PART), b16),
            pltpu.VMEM((nz - 1, TILE, PART), b16),
            longs,
            rings,
            pltpu.SemaphoreType.DMA((2,)),
            pltpu.SemaphoreType.DMA((3,)),
            pltpu.SemaphoreType.DMA((3,)),
            pltpu.SemaphoreType.DMA((15,)),
            pltpu.SemaphoreType.DMA((15,)),
            pltpu.SemaphoreType.DMA((2, copies)),
            pltpu.SemaphoreType.DMA((2, copies)),
            pltpu.SemaphoreType.DMA((2, 7)),
            pltpu.SemaphoreType.DMA((2, 7)),
            pltpu.SemaphoreType.DMA((RINGS, 6)),
            pltpu.SemaphoreType.DMA((RINGS, 6)),
        ],
        compiler_params=pltpu.CompilerParams(
            collective_id=0, has_side_effects=True, vmem_limit_bytes=56 * 1024 * 1024),
        cost_estimate=pl.CostEstimate(flops=4_500_000_000, bytes_accessed=8_000_000, transcendentals=300_000),
    )(image_features, text_features, image_weight, text_weight, partner)
    return pl.pallas_call(
        hand_over,
        out_shape=[jax.ShapeDtypeStruct(out.shape, out.dtype) for out in outs],
        in_specs=[vmem] * 4,
        out_specs=[vmem] * 4,
    )(*outs)


def solution(mesh):
    in_specs = (
        P(("wide", "narrow"), None),
        P(("wide", "narrow"), None),
        P(),
        P(),
        P("wide", "narrow"),
    )
    out_specs = (
        P(("wide", "narrow"), None),
        P(("wide", "narrow"), None),
        P("wide", "narrow"),
        P("wide", "narrow"),
    )
    nz = mesh.shape["wide"] // (NX * NYH)
    return jax.shard_map(
        functools.partial(local, nz), mesh=mesh, in_specs=in_specs, out_specs=out_specs, check_vma=False)
```
